128 devices in a mesh: queue: 8 (over z_lo, y), seq: 16 (over z_hi, x, core).
Axes of the slice: x: 4, y: 4, z: 4 (z_hi: 2, z_lo: 2; z = z_hi * 2 + z_lo), core: 2. Of those that a mesh axis runs over, the one named last changes fastest.
Arguments:
- latents: bfloat16 [8, 4, 128, 5120], P('queue', None, 'seq'), may hold values from -6 to 6
- steps: int32 [8], P('queue'), may hold values from 0 to 49
- leaving: int32 [8], P('queue'), may hold values from 0 to 3
- fresh: bfloat16 [128, 5120], P('seq'), may hold values from -6 to 6
- mod_table: float32 [50, 15360], replicated, may hold values from -4 to 4
- w_qkv: bfloat16 [5120, 3, 4096], P(None, None, 'seq'), may hold values from -0.078125 to 0.078125
- q_gain: float32 [4096], P('seq'), may hold values from 0.5 to 16
- k_gain: float32 [4096], P('seq'), may hold values from 0.5 to 16
- w_out: bfloat16 [4096, 5120], P('seq'), may hold values from -0.09375 to 0.09375
Outputs:
- queue_next: bfloat16 [8, 4, 128, 5120], P('queue', None, 'seq')
The draws below stay inside these ranges and needn't reach their ends.
All inputs are finite; a program needn't handle non-finite values.
Results may differ from the reference program's by a relative error of at most 0.017.
Values may be sent and summed in bfloat16 or wider, within the bound.
No kernel may reach another device: no remote copies, remote signals or barrier semaphores. Data moves between devices by JAX's collectives and lax.ppermute only.
A program may use at most 128 MiB of HBM per device.

```python
import math
import jax
import jax.numpy as jnp
from jax import lax

D = 5120
HEAD_DIM = 128
HEADS = 32
LEVELS = 50
FRAMES = 4
FRAME_TOK = 128
PARTS_SIZE = 8
N_SEQ = 16


def draw_q_gain(key, part):
    key = jax.random.fold_in(key, 17)
    count = HEADS * HEAD_DIM
    return jnp.exp(jax.random.uniform(key, (count,), jnp.float32, math.log(0.7), math.log(2.5)))


def draw_k_gain(key, part):
    key = jax.random.fold_in(key, 29)
    count = HEADS * HEAD_DIM
    return jnp.exp(jax.random.uniform(key, (count,), jnp.float32, math.log(0.7), math.log(2.5)))


def plant(result, own_key, low, high):
    longest = result.shape.index(max(result.shape))
    spots = []
    for shift in (0, 1):
        where = [jax.random.randint(jax.random.fold_in(own_key, axis), (), 0, length) for axis, length in enumerate(result.shape)]
        where[longest] = (where[longest] + shift) % result.shape[longest]
        spots.append(tuple(where))
    return result.at[spots[0]].set(low).at[spots[1]].set(high)


def shard_levels(key, dims, shards, smallest, high):
    level, own = 1.0, jax.random.fold_in(key, 6)
    for position, shards_of in shards:
        draws = jnp.exp(jax.random.uniform(jax.random.fold_in(own, position), (shards_of,), jnp.float32, smallest / len(shards), high / len(shards)))
        level = level * jnp.repeat(draws, dims[position] // shards_of).reshape([-1 if axis == position else 1 for axis in range(len(dims))])
    return level


def bell_draw(rng, extent, deviation, most, shards=(), kind=jnp.bfloat16):
    values = deviation * jax.random.normal(rng, extent, jnp.float32)
    if shards:
        values = values * shard_levels(rng, extent, shards, -0.22, 0.18)
    return jnp.clip(values, -most, most).astype(kind)


def setup_inputs(seed: int = 0) -> dict:
    streams_of = jax.random.split(jax.random.key(seed), 10)
    return {
        "latents": bell_draw(streams_of[0], (PARTS_SIZE, FRAMES, FRAME_TOK, D), 1.0, 6.0, ((0, 8), (2, 16))),
        "steps": plant(jax.random.randint(streams_of[1], (PARTS_SIZE,), 0, LEVELS), jax.random.fold_in(streams_of[1], 1), 0, LEVELS - 1).astype(jnp.int32),
        "leaving": plant(jax.random.randint(streams_of[2], (PARTS_SIZE,), 0, FRAMES), jax.random.fold_in(streams_of[2], 1), 0, FRAMES - 1).astype(jnp.int32),
        "fresh": bell_draw(streams_of[3], (FRAME_TOK, D), 1.0, 6.0, ((0, 16),)),
        "mod_table": bell_draw(streams_of[4], (LEVELS, 3 * D), 0.7, 4.0, (), jnp.float32),
        "w_qkv": bell_draw(streams_of[5], (D, 3, HEADS * HEAD_DIM), D ** -0.5, 0.078125, ((2, 16),)),
        "q_gain": draw_q_gain(jax.random.fold_in(streams_of[9], 71), 0),
        "k_gain": draw_k_gain(jax.random.fold_in(streams_of[9], 71), 0),
        "w_out": bell_draw(streams_of[8], (HEADS * HEAD_DIM, D), (HEADS * HEAD_DIM) ** -0.5, 0.09375, ((0, 16),)),
    }


def layer_norm_mod(rows, shift, scale):
    values = rows.astype(jnp.float32)
    mean = lax.optimization_barrier(jnp.mean(values, axis=-1, keepdims=True))
    centred = values - mean
    var = lax.optimization_barrier(jnp.mean(centred * centred, axis=-1, keepdims=True))
    return (centred * lax.rsqrt(var + 1e-06) * (1.0 + scale) + shift).astype(jnp.bfloat16)

def head_norm(values, gain):
    power = lax.optimization_barrier(jnp.mean(values * values, axis=-1, keepdims=True))
    return values * lax.rsqrt(power + 1e-06) * gain

def reference(latents, steps, leaving, fresh, mod_table, w_qkv, q_gain, k_gain, w_out):
    width = HEADS * HEAD_DIM
    length = FRAMES * FRAME_TOK
    group = width // N_SEQ
    modrows = mod_table[steps]

    def one(item):
        block, modrow = item
        shift = modrow[:D]
        scale = modrow[D:2 * D]
        gate = modrow[2 * D:]
        rows = block.reshape(length, D)
        normed = layer_norm_mod(rows, shift, scale)
        qkv = jnp.dot(normed, w_qkv.reshape(D, 3 * width), preferred_element_type=jnp.float32)
        qkv = qkv.reshape(length, 3, HEADS, HEAD_DIM)
        query = head_norm(qkv[:, 0], q_gain.reshape(HEADS, HEAD_DIM)).astype(jnp.bfloat16)
        keys = head_norm(qkv[:, 1], k_gain.reshape(HEADS, HEAD_DIM)).astype(jnp.bfloat16)
        values = qkv[:, 2].astype(jnp.bfloat16)
        scores = jnp.einsum('qhd,khd->hqk', query.astype(jnp.float32), keys.astype(jnp.float32)) * HEAD_DIM ** (-0.5)
        top = lax.optimization_barrier(jnp.max(scores, axis=-1, keepdims=True))
        expo = jnp.exp(scores - top)
        total = lax.optimization_barrier(jnp.sum(expo, axis=-1, keepdims=True))
        prob = (expo / total).astype(jnp.bfloat16)
        attn = jnp.einsum('hqk,khd->qhd', prob.astype(jnp.float32), values.astype(jnp.float32))
        attn = attn.astype(jnp.bfloat16).reshape(length, width)
        proj = jnp.zeros((length, D), jnp.float32)
        for index in range(N_SEQ):
            piece = jnp.dot(attn[:, index * group:(index + 1) * group], w_out[index * group:(index + 1) * group], preferred_element_type=jnp.float32)
            proj = proj + lax.optimization_barrier(piece.astype(jnp.bfloat16)).astype(jnp.float32)
        updated = (rows.astype(jnp.float32) + gate * proj).astype(jnp.bfloat16)
        return updated.reshape(FRAMES, FRAME_TOK, D)
    updated = lax.map(one, (latents, modrows))
    parts_all = updated.shape[0]
    handed = updated[jnp.arange(parts_all), leaving]
    incoming = jnp.concatenate([fresh[None], handed[:-1]], axis=0)
    mask = jnp.arange(FRAMES)[None, :] == leaving[:, None]
    return jnp.where(mask[:, :, None, None], incoming[:, None], updated)
```

```python
import functools

import jax
import jax.numpy as jnp
from jax import lax
from jax.experimental import pallas as pl
from jax.experimental.pallas import tpu as pltpu
from jax.sharding import PartitionSpec as P

HEAD_DIM = 128
Z_CHIPS, X_CHIPS, CORES = 2, 4, 2
MIB = 1 << 20


def hop(value, dz=0, dx=0, dc=0):
    pairs = []
    for z in range(Z_CHIPS):
        for x in range(X_CHIPS):
            for c in range(CORES):
                to_z, to_x, to_c = (z + dz) % Z_CHIPS, (x + dx) % X_CHIPS, (c + dc) % CORES
                pairs.append(((z * X_CHIPS + x) * CORES + c, (to_z * X_CHIPS + to_x) * CORES + to_c))
    return lax.ppermute(value, "seq", pairs)


def from_behind(x, axis, by):
    count = lax.axis_size(axis)
    pairs = [(i, i + by) for i in range(count) if 0 <= i + by < count]
    return lax.ppermute(x, axis, pairs)


def layer_norm_mod(rows, shift, scale):
    values = rows.astype(jnp.float32)
    mean = jnp.mean(values, axis=-1, keepdims=True)
    centred = values - mean
    var = jnp.mean(centred * centred, axis=-1, keepdims=True)
    return (centred * lax.rsqrt(var + 1e-06) * (1.0 + scale) + shift).astype(jnp.bfloat16)


def qkv_kernel(pieces, *refs):
    xs, (w_mine, w_other, gains, q_ref, kv_ref, rows_ref) = refs[:pieces], refs[pieces:]
    step = pl.program_id(0)
    rows = xs[0].shape[0]

    @pl.when(step == 0)
    def _():
        for i, x in enumerate(xs):
            rows_ref[i * rows : (i + 1) * rows, :] = x[...]

    def project(w):
        return jnp.dot(rows_ref[...], w[0], preferred_element_type=jnp.float32)

    def normed(values, gain):
        out = []
        for head in range(values.shape[1] // HEAD_DIM):
            part = values[:, head * HEAD_DIM : (head + 1) * HEAD_DIM]
            power = jnp.mean(part * part, axis=-1, keepdims=True)
            out.append(part * lax.rsqrt(power + 1e-06) * gain[:, head * HEAD_DIM : (head + 1) * HEAD_DIM])
        return jnp.concatenate(out, axis=1).astype(jnp.bfloat16)

    for owner, w in enumerate((w_mine, w_other)):
        @pl.when(step == 3 * owner)
        def _(owner=owner, w=w):
            q_ref[owner] = normed(project(w), gains[2 * owner : 2 * owner + 1, :])

        @pl.when(step == 3 * owner + 1)
        def _(owner=owner, w=w):
            kv_ref[2 * owner] = normed(project(w), gains[2 * owner + 1 : 2 * owner + 2, :])

        @pl.when(step == 3 * owner + 2)
        def _(owner=owner, w=w):
            kv_ref[2 * owner + 1] = project(w).astype(jnp.bfloat16)


def qkv_call(xs, w_mine, w_other, gains):
    pieces = len(xs)
    rows, width = xs[0].shape
    cols = w_mine.shape[2]
    total = rows * pieces
    whole = lambda shape: pl.BlockSpec(shape, lambda i: (0,) * len(shape))
    return pl.pallas_call(
        functools.partial(qkv_kernel, pieces),
        grid=(6,),
        in_specs=[whole((rows, width))] * pieces
        + [
            pl.BlockSpec((1, width, cols), lambda i: (jnp.minimum(i, 2), 0, 0)),
            pl.BlockSpec((1, width, cols), lambda i: (jnp.maximum(i - 3, 0), 0, 0)),
            whole(gains.shape),
        ],
        out_specs=[whole((2, total, cols)), whole((4, total, cols))],
        out_shape=[
            jax.ShapeDtypeStruct((2, total, cols), jnp.bfloat16),
            jax.ShapeDtypeStruct((4, total, cols), jnp.bfloat16),
        ],
        scratch_shapes=[pltpu.VMEM((total, width), jnp.bfloat16)],
        compiler_params=pltpu.CompilerParams(vmem_limit_bytes=40 * MIB),
        cost_estimate=pl.CostEstimate(
            flops=2 * total * width * cols * 6, bytes_accessed=12 * width * cols, transcendentals=0
        ),
    )(*xs, w_mine, w_other, gains)


def attend_kernel(pieces, q_ref, kv_ref, kv_far, w_mine, w_other, *refs):
    outs, attn_ref = refs[:pieces], refs[pieces]
    rows = outs[0].shape[0]
    contract = (((1,), (1,)), ((), ()))

    @pl.when(pl.program_id(0) == 0)
    def _():
        cols = q_ref.shape[2]
        for owner in range(2):
            for head in range(cols // HEAD_DIM):
                span = slice(head * HEAD_DIM, (head + 1) * HEAD_DIM)
                query = q_ref[owner, :, span]
                near, far = 2 * owner, 2 * (1 - owner)
                scores = jnp.concatenate(
                    [
                        lax.dot_general(query, kv_ref[near, :, span], contract, preferred_element_type=jnp.float32),
                        lax.dot_general(query, kv_far[far, :, span], contract, preferred_element_type=jnp.float32),
                    ],
                    axis=1,
                ) * HEAD_DIM ** (-0.5)
                top = jnp.max(scores, axis=-1, keepdims=True)
                expo = jnp.exp(scores - top)
                total = jnp.sum(expo, axis=-1, keepdims=True)
                prob = (expo / total).astype(jnp.bfloat16)
                half = kv_ref.shape[1]
                value = jnp.dot(prob[:, :half], kv_ref[near + 1, :, span], preferred_element_type=jnp.float32)
                value += jnp.dot(prob[:, half:], kv_far[far + 1, :, span], preferred_element_type=jnp.float32)
                at = owner * cols + head * HEAD_DIM
                attn_ref[:, at : at + HEAD_DIM] = value.astype(jnp.bfloat16)

    cols = w_mine.shape[0]
    part = jnp.dot(attn_ref[:, :cols], w_mine[...], preferred_element_type=jnp.float32)
    part += jnp.dot(attn_ref[:, cols:], w_other[...], preferred_element_type=jnp.float32)
    part = part.astype(jnp.bfloat16)
    for i, out in enumerate(outs):
        out[...] = part[i * rows : (i + 1) * rows, :]


def attend_call(q, kv, kv_far, w_mine, w_other, pieces):
    total = q.shape[1]
    rows = total // pieces
    cols, width = w_mine.shape
    block = 1024
    whole = lambda shape: pl.BlockSpec(shape, lambda i: (0,) * len(shape))
    return pl.pallas_call(
        functools.partial(attend_kernel, pieces),
        grid=(width // block,),
        in_specs=[
            whole(q.shape),
            whole(kv.shape),
            whole(kv_far.shape),
            pl.BlockSpec((cols, block), lambda i: (0, i)),
            pl.BlockSpec((cols, block), lambda i: (0, i)),
        ],
        out_specs=[pl.BlockSpec((rows, block), lambda i: (0, i))] * pieces,
        out_shape=[jax.ShapeDtypeStruct((rows, width), jnp.bfloat16)] * pieces,
        scratch_shapes=[pltpu.VMEM((total, 2 * cols), jnp.bfloat16)],
        compiler_params=pltpu.CompilerParams(vmem_limit_bytes=32 * MIB),
        cost_estimate=pl.CostEstimate(
            flops=4 * total * cols * width + 16 * total * total * cols,
            bytes_accessed=4 * cols * width,
            transcendentals=8 * total * total,
        ),
    )(q, kv, kv_far, w_mine, w_other)


def body(latents, steps, leaving, fresh, mod_table, w_qkv, q_gain, k_gain, w_out):
    _, frames, local_rows, width = latents.shape
    rows = frames * local_rows
    modrow = lax.dynamic_slice_in_dim(mod_table, steps[0], 1, axis=0)
    shift, scale, gate = modrow[:, :width], modrow[:, width : 2 * width], modrow[:, 2 * width :]
    own = latents.reshape(rows, width)
    normed = layer_norm_mod(own, shift, scale)

    w_mine = w_qkv.transpose(1, 0, 2)
    w_other = hop(w_mine, dc=1)
    gain_mine = jnp.stack([q_gain, k_gain])
    gains = jnp.concatenate([gain_mine, hop(gain_mine, dc=1)], axis=0)
    out_other = hop(w_out, dc=1)

    left = hop(normed, dx=1)
    right = hop(normed, dx=-1)
    far = hop(normed, dz=1)
    across = hop(normed, dx=2)
    far_left = hop(left, dz=1)
    far_right = hop(right, dz=1)
    far_across = hop(far, dx=2)
    xs = [normed, left, right, far, across, far_left, far_right, far_across]

    q, kv = qkv_call(xs, w_mine, w_other, gains)
    kv_far = hop(kv, dc=1)
    parts = attend_call(q, kv, kv_far, w_out, out_other, len(xs))
    p_own, p_left, p_right, p_far, p_across, p_far_left, p_far_right, p_far_across = parts

    def add(a, b):
        return (a.astype(jnp.float32) + b.astype(jnp.float32)).astype(jnp.bfloat16)

    s_left = add(p_left, hop(p_far_left, dz=1))
    s_right = add(p_right, hop(p_far_right, dz=1))
    s_far = add(p_far, hop(p_far_across, dx=2))
    arrived = [hop(p_across, dx=2), hop(s_left, dx=-1), hop(s_right, dx=1), hop(s_far, dz=1)]
    proj = p_own.astype(jnp.float32)
    for piece in arrived:
        proj = proj + piece.astype(jnp.float32)

    updated = (own.astype(jnp.float32) + gate * proj).astype(jnp.bfloat16).reshape(frames, local_rows, width)
    handed = lax.dynamic_slice_in_dim(updated, leaving[0], 1, axis=0)[0]
    arriving = from_behind(handed, "queue", 1)
    first = jnp.where(lax.axis_index("queue") == 0, fresh, arriving)
    select = jnp.arange(frames) == leaving[0]
    return jnp.where(select[:, None, None], first[None], updated)[None]


def solution(mesh):
    return jax.shard_map(
        body,
        mesh=mesh,
        in_specs=(
            P("queue", None, "seq", None),
            P("queue"),
            P("queue"),
            P("seq", None),
            P(),
            P(None, None, "seq"),
            P("seq"),
            P("seq"),
            P("seq", None),
        ),
        out_specs=P("queue", None, "seq", None),
        check_vma=False,
    )
```

```python
import functools

import jax
import jax.numpy as jnp
from jax import lax
from jax.experimental import pallas as pl
from jax.experimental.pallas import tpu as pltpu
from jax.sharding import PartitionSpec as P

HEAD_DIM = 128
Z_CHIPS, X_CHIPS, CORES = 2, 4, 2
MIB = 1 << 20
ANY = pl.BlockSpec(memory_space=pl.ANY)
VMEM = pl.BlockSpec(memory_space=pltpu.VMEM)
SMEM = pl.BlockSpec(memory_space=pltpu.SMEM)


def hop(value, dz=0, dx=0, dc=0):
    pairs = []
    for z in range(Z_CHIPS):
        for x in range(X_CHIPS):
            for c in range(CORES):
                to_z, to_x, to_c = (z + dz) % Z_CHIPS, (x + dx) % X_CHIPS, (c + dc) % CORES
                pairs.append(((z * X_CHIPS + x) * CORES + c, (to_z * X_CHIPS + to_x) * CORES + to_c))
    return lax.ppermute(value, "seq", pairs)


def from_behind(x, axis, by):
    count = lax.axis_size(axis)
    pairs = [(i, i + by) for i in range(count) if 0 <= i + by < count]
    return lax.ppermute(x, axis, pairs)


def norm_kernel(step, x_ref, table, out_ref, gate_ref, row, sem):
    width = x_ref.shape[-1]
    copy = pltpu.make_async_copy(table.at[pl.ds(step[0], 1), :], row, sem)
    copy.start()
    values = x_ref[...].astype(jnp.float32)
    mean = jnp.mean(values, axis=-1, keepdims=True)
    centred = values - mean
    var = jnp.mean(centred * centred, axis=-1, keepdims=True)
    scaled = centred * lax.rsqrt(var + 1e-06)
    copy.wait()
    shift, scale = row[:, :width], row[:, width : 2 * width]
    out_ref[...] = (scaled * (1.0 + scale) + shift).astype(jnp.bfloat16)
    gate_ref[...] = row[:, 2 * width :]


def norm_call(step, x, table):
    rows, width = x.shape
    return pl.pallas_call(
        norm_kernel,
        in_specs=[SMEM, VMEM, ANY],
        out_specs=[VMEM, VMEM],
        out_shape=[
            jax.ShapeDtypeStruct((rows, width), jnp.bfloat16),
            jax.ShapeDtypeStruct((1, width), jnp.float32),
        ],
        scratch_shapes=[pltpu.VMEM((1, 3 * width), jnp.float32), pltpu.SemaphoreType.DMA],
        compiler_params=pltpu.CompilerParams(vmem_limit_bytes=8 * MIB),
        cost_estimate=pl.CostEstimate(flops=10 * rows * width, bytes_accessed=4 * rows * width, transcendentals=0),
    )(step, x, pltpu.with_memory_space_constraint(table, pltpu.HBM))


def head_norm(values, gain):
    out = []
    for at in range(0, values.shape[1], HEAD_DIM):
        part = values[:, at : at + HEAD_DIM]
        power = jnp.mean(part * part, axis=-1, keepdims=True)
        out.append(part * lax.rsqrt(power + 1e-06) * gain[:, at : at + HEAD_DIM])
    return jnp.concatenate(out, axis=1)


def project(i, rows_ref, weights, gains, q_ref, kv_ref):
    owner, kind = divmod(i, 3)
    acc = jnp.dot(rows_ref[...], weights[i], preferred_element_type=jnp.float32)
    if kind < 2:
        acc = head_norm(acc, gains[2 * owner + kind][...])
    if kind == 0:
        q_ref[owner] = acc.astype(jnp.bfloat16)
    else:
        kv_ref[2 * owner + kind - 1] = acc.astype(jnp.bfloat16)


def gather_rows(xs, rows_ref):
    rows = xs[0].shape[0]
    for i, x in enumerate(xs):
        rows_ref[i * rows : (i + 1) * rows, :] = x[...]


def first_kernel(pieces, *refs):
    xs, gains = refs[:pieces], refs[pieces : pieces + 4]
    w_mine, w_other, q_ref, kv_ref, held, rows_ref, sems = refs[pieces + 4 :]
    copies = []
    for i in range(6):
        copies.append(pltpu.make_async_copy((w_mine, w_other)[i // 3].at[i % 3], held.at[i], sems.at[i]))
        copies[i].start()
    gather_rows(xs, rows_ref)
    for i in range(6):
        copies[i].wait()
        project(i, rows_ref, held, gains, q_ref, kv_ref)


def rest_kernel(pieces, *refs):
    xs, gains = refs[:pieces], refs[pieces : pieces + 4]
    held, q_ref, kv_ref, rows_ref = refs[pieces + 4 :]
    gather_rows(xs, rows_ref)
    for i in range(6):
        project(i, rows_ref, held, gains, q_ref, kv_ref)


def qkv_shapes(total, cols):
    return [
        jax.ShapeDtypeStruct((2, total, cols), jnp.bfloat16),
        jax.ShapeDtypeStruct((4, total, cols), jnp.bfloat16),
    ]


def first_call(xs, gains, w_mine, w_other):
    pieces = len(xs)
    rows, width = xs[0].shape
    total, cols = rows * pieces, w_mine.shape[2]
    return pl.pallas_call(
        functools.partial(first_kernel, pieces),
        in_specs=[VMEM] * (pieces + 4) + [ANY, ANY],
        out_specs=[VMEM] * 3,
        out_shape=qkv_shapes(total, cols) + [pltpu.VMEM((6, width, cols), jnp.bfloat16)],
        scratch_shapes=[pltpu.VMEM((total, width), jnp.bfloat16), pltpu.SemaphoreType.DMA((6,))],
        compiler_params=pltpu.CompilerParams(vmem_limit_bytes=24 * MIB),
        cost_estimate=pl.CostEstimate(
            flops=12 * total * width * cols, bytes_accessed=12 * width * cols, transcendentals=0
        ),
    )(
        *xs,
        *gains,
        pltpu.with_memory_space_constraint(w_mine, pltpu.HBM),
        pltpu.with_memory_space_constraint(w_other, pltpu.HBM),
    )


def rest_call(xs, gains, held):
    pieces = len(xs)
    rows, width = xs[0].shape
    total, cols = rows * pieces, held.shape[2]
    return pl.pallas_call(
        functools.partial(rest_kernel, pieces),
        in_specs=[VMEM] * (pieces + 5),
        out_specs=[VMEM] * 2,
        out_shape=qkv_shapes(total, cols),
        scratch_shapes=[pltpu.VMEM((total, width), jnp.bfloat16)],
        compiler_params=pltpu.CompilerParams(vmem_limit_bytes=24 * MIB),
        cost_estimate=pl.CostEstimate(
            flops=12 * total * width * cols, bytes_accessed=12 * width * cols, transcendentals=0
        ),
    )(*xs, *gains, pltpu.with_memory_space_constraint(held, pltpu.VMEM))


def attend_kernel(pieces, q_a, q_b, kv_a, kv_b, far_a, far_b, w_mine, w_other, *refs):
    outs, (q_ref, kv_ref, attn_ref) = refs[:pieces], refs[pieces:]
    rows = outs[0].shape[0]
    cols = q_a.shape[2]
    contract = (((1,), (1,)), ((), ()))

    @pl.when(pl.program_id(0) == 0)
    def _():
        cut, half = q_a.shape[1], q_ref.shape[1]
        for owner in range(2):
            q_ref[owner, :cut, :] = q_a[owner]
            q_ref[owner, cut:, :] = q_b[owner]
            for kind in range(2):
                near, far = 2 * owner + kind, 2 * (1 - owner) + kind
                kv_ref[near, :cut, :] = kv_a[near]
                kv_ref[near, cut:half, :] = kv_b[near]
                kv_ref[near, half : half + cut, :] = far_a[far]
                kv_ref[near, half + cut :, :] = far_b[far]
        for owner in range(2):
            for at in range(0, cols, HEAD_DIM):
                span = slice(at, at + HEAD_DIM)
                scores = lax.dot_general(
                    q_ref[owner, :, span], kv_ref[2 * owner, :, span], contract, preferred_element_type=jnp.float32
                ) * HEAD_DIM ** (-0.5)
                top = jnp.max(scores, axis=-1, keepdims=True)
                expo = jnp.exp(scores - top)
                total = jnp.sum(expo, axis=-1, keepdims=True)
                prob = (expo * (1.0 / total)).astype(jnp.bfloat16)
                value = jnp.dot(prob, kv_ref[2 * owner + 1, :, span], preferred_element_type=jnp.float32)
                attn_ref[:, owner * cols + at : owner * cols + at + HEAD_DIM] = value.astype(jnp.bfloat16)

    part = jnp.dot(attn_ref[:, :cols], w_mine[...], preferred_element_type=jnp.float32)
    part += jnp.dot(attn_ref[:, cols:], w_other[...], preferred_element_type=jnp.float32)
    part = part.astype(jnp.bfloat16)
    for i, out in enumerate(outs):
        out[...] = part[i * rows : (i + 1) * rows, :]


def attend_call(q_a, q_b, kv_a, kv_b, far_a, far_b, w_mine, w_other, pieces):
    total = q_a.shape[1] + q_b.shape[1]
    rows = total // pieces
    cols, width = w_mine.shape
    block = 1024
    whole = lambda x: pl.BlockSpec(x.shape, lambda i: (0,) * x.ndim)
    operands = (q_a, q_b, kv_a, kv_b, far_a, far_b)
    return pl.pallas_call(
        functools.partial(attend_kernel, pieces),
        grid=(width // block,),
        in_specs=[whole(x) for x in operands] + [pl.BlockSpec((cols, block), lambda i: (0, i))] * 2,
        out_specs=[pl.BlockSpec((rows, block), lambda i: (0, i))] * pieces,
        out_shape=[jax.ShapeDtypeStruct((rows, width), jnp.bfloat16)] * pieces,
        scratch_shapes=[
            pltpu.VMEM((2, total, cols), jnp.bfloat16),
            pltpu.VMEM((4, 2 * total, cols), jnp.bfloat16),
            pltpu.VMEM((total, 2 * cols), jnp.bfloat16),
        ],
        compiler_params=pltpu.CompilerParams(vmem_limit_bytes=32 * MIB),
        cost_estimate=pl.CostEstimate(
            flops=4 * total * cols * width + 16 * total * total * cols,
            bytes_accessed=4 * cols * width,
            transcendentals=8 * total * total,
        ),
    )(*operands, w_mine, w_other)


def body(latents, steps, leaving, fresh, mod_table, w_qkv, q_gain, k_gain, w_out):
    _, frames, local_rows, width = latents.shape
    rows = frames * local_rows
    own = latents.reshape(rows, width)
    normed, gate = norm_call(steps, own, mod_table)

    w_mine = w_qkv.transpose(1, 0, 2)
    q_gain, k_gain = q_gain[None], k_gain[None]
    q_other, k_other = hop(q_gain, dc=1), hop(k_gain, dc=1)
    gains = [q_gain, k_gain, q_other, k_other]
    w_send, out_send, _, _ = lax.optimization_barrier((w_mine, w_out, q_other, k_other))
    w_other = hop(w_send, dc=1)
    out_other = hop(out_send, dc=1)

    left = hop(normed, dx=1)
    right = hop(normed, dx=-1)
    far = hop(normed, dz=1)
    across = hop(normed, dx=2)
    far_left = hop(left, dz=1)
    far_right = hop(right, dz=1)
    far_across = hop(far, dx=2)

    q_a, kv_a, held = first_call([normed, left, right, far, across], gains, w_mine, w_other)
    far_a = hop(kv_a, dc=1)
    q_b, kv_b = rest_call([far_left, far_right, far_across], gains, held)
    far_b = hop(kv_b, dc=1)
    parts = attend_call(q_a, q_b, kv_a, kv_b, far_a, far_b, w_out, out_other, 8)
    p_own, p_left, p_right, p_far, p_across, p_far_left, p_far_right, p_far_across = parts

    def add(a, b):
        return (a.astype(jnp.float32) + b.astype(jnp.float32)).astype(jnp.bfloat16)

    s_left = add(p_left, hop(p_far_left, dz=1))
    s_right = add(p_right, hop(p_far_right, dz=1))
    s_far = add(p_far, hop(p_far_across, dx=2))
    arrived = [hop(p_across, dx=2), hop(s_left, dx=-1), hop(s_right, dx=1), hop(s_far, dz=1)]
    proj = p_own.astype(jnp.float32)
    for piece in arrived:
        proj = proj + piece.astype(jnp.float32)

    updated = (own.astype(jnp.float32) + gate * proj).astype(jnp.bfloat16).reshape(frames, local_rows, width)
    handed = lax.dynamic_slice_in_dim(updated, leaving[0], 1, axis=0)[0]
    arriving = from_behind(handed, "queue", 1)
    first = jnp.where(lax.axis_index("queue") == 0, fresh, arriving)
    select = jnp.arange(frames) == leaving[0]
    return jnp.where(select[:, None, None], first[None], updated)[None]


def solution(mesh):
    return jax.shard_map(
        body,
        mesh=mesh,
        in_specs=(
            P("queue", None, "seq", None),
            P("queue"),
            P("queue"),
            P("seq", None),
            P(),
            P(None, None, "seq"),
            P("seq"),
            P("seq"),
            P("seq", None),
        ),
        out_specs=P("queue", None, "seq", None),
        check_vma=False,
    )
```

```python
import functools

import jax
import jax.numpy as jnp
from jax import lax
from jax.experimental import pallas as pl
from jax.experimental.pallas import tpu as pltpu
from jax.sharding import PartitionSpec as P

HEAD_DIM = 128
Z_CHIPS, X_CHIPS, CORES = 2, 4, 2
MIB = 1 << 20
ANY = pl.BlockSpec(memory_space=pl.ANY)
VMEM = pl.BlockSpec(memory_space=pltpu.VMEM)
SMEM = pl.BlockSpec(memory_space=pltpu.SMEM)


def hop(value, dz=0, dx=0, dc=0):
    pairs = []
    for z in range(Z_CHIPS):
        for x in range(X_CHIPS):
            for c in range(CORES):
                to_z, to_x, to_c = (z + dz) % Z_CHIPS, (x + dx) % X_CHIPS, (c + dc) % CORES
                pairs.append(((z * X_CHIPS + x) * CORES + c, (to_z * X_CHIPS + to_x) * CORES + to_c))
    return lax.ppermute(value, "seq", pairs)


def from_behind(x, axis, by):
    count = lax.axis_size(axis)
    pairs = [(i, i + by) for i in range(count) if 0 <= i + by < count]
    return lax.ppermute(x, axis, pairs)


def norm_kernel(step, x_hbm, table, q_hbm, k_hbm, out_ref, gate_ref, gain_ref, x_ref, row, q_ref, k_ref, sems):
    width = x_hbm.shape[-1]
    moves = [(x_hbm, x_ref), (table.at[pl.ds(step[0], 1), :], row), (q_hbm, q_ref), (k_hbm, k_ref)]
    copies = [pltpu.make_async_copy(src, dst, sems.at[i]) for i, (src, dst) in enumerate(moves)]
    for copy in copies:
        copy.start()
    copies[0].wait()
    values = x_ref[...].astype(jnp.float32)
    mean = jnp.mean(values, axis=-1, keepdims=True)
    centred = values - mean
    var = jnp.mean(centred * centred, axis=-1, keepdims=True)
    scaled = centred * lax.rsqrt(var + 1e-06)
    for copy in copies[1:]:
        copy.wait()
    shift, scale = row[:, :width], row[:, width : 2 * width]
    out_ref[...] = (scaled * (1.0 + scale) + shift).astype(jnp.bfloat16)
    gate_ref[...] = row[:, 2 * width :]
    gain_ref[0:1, :] = q_ref[...]
    gain_ref[1:2, :] = k_ref[...]


def norm_call(step, x, table, q_gain, k_gain):
    rows, width = x.shape
    cols = q_gain.shape[1]
    in_hbm = lambda array: pltpu.with_memory_space_constraint(array, pltpu.HBM)
    return pl.pallas_call(
        norm_kernel,
        in_specs=[SMEM] + [ANY] * 4,
        out_specs=[VMEM] * 3,
        out_shape=[
            jax.ShapeDtypeStruct((rows, width), jnp.bfloat16),
            jax.ShapeDtypeStruct((1, width), jnp.float32),
            jax.ShapeDtypeStruct((2, cols), jnp.float32),
        ],
        scratch_shapes=[
            pltpu.VMEM((rows, width), jnp.bfloat16),
            pltpu.VMEM((1, 3 * width), jnp.float32),
            pltpu.VMEM((1, cols), jnp.float32),
            pltpu.VMEM((1, cols), jnp.float32),
            pltpu.SemaphoreType.DMA((4,)),
        ],
        compiler_params=pltpu.CompilerParams(vmem_limit_bytes=8 * MIB),
        cost_estimate=pl.CostEstimate(flops=10 * rows * width, bytes_accessed=4 * rows * width, transcendentals=0),
    )(step, in_hbm(x), in_hbm(table), in_hbm(q_gain), in_hbm(k_gain))


def head_norm(values, gain):
    out = []
    for at in range(0, values.shape[1], HEAD_DIM):
        part = values[:, at : at + HEAD_DIM]
        power = jnp.mean(part * part, axis=-1, keepdims=True)
        out.append(part * lax.rsqrt(power + 1e-06) * gain[:, at : at + HEAD_DIM])
    return jnp.concatenate(out, axis=1)


def project(i, rows_ref, weights, gains, q_ref, kv_ref):
    owner, kind = divmod(i, 3)
    acc = jnp.dot(rows_ref[...], weights[i], preferred_element_type=jnp.float32)
    if kind < 2:
        acc = head_norm(acc, gains[owner][kind : kind + 1, :])
    if kind == 0:
        q_ref[owner] = acc.astype(jnp.bfloat16)
    else:
        kv_ref[2 * owner + kind - 1] = acc.astype(jnp.bfloat16)


def gather_rows(xs, rows_ref):
    rows = xs[0].shape[0]
    for i, x in enumerate(xs):
        rows_ref[i * rows : (i + 1) * rows, :] = x[...]


def first_kernel(pieces, *refs):
    xs, gains = refs[:pieces], refs[pieces : pieces + 2]
    w_mine, w_other, q_ref, kv_ref, held, rows_ref, sems = refs[pieces + 2 :]
    copies = []
    for i in range(6):
        copies.append(pltpu.make_async_copy((w_mine, w_other)[i // 3].at[i % 3], held.at[i], sems.at[i]))
        copies[i].start()
    gather_rows(xs, rows_ref)
    for i in range(6):
        copies[i].wait()
        project(i, rows_ref, held, gains, q_ref, kv_ref)


def rest_kernel(pieces, *refs):
    xs, gains = refs[:pieces], refs[pieces : pieces + 2]
    held, q_ref, kv_ref, rows_ref = refs[pieces + 2 :]
    gather_rows(xs, rows_ref)
    for i in range(6):
        project(i, rows_ref, held, gains, q_ref, kv_ref)


def qkv_shapes(total, cols):
    return [
        jax.ShapeDtypeStruct((2, total, cols), jnp.bfloat16),
        jax.ShapeDtypeStruct((4, total, cols), jnp.bfloat16),
    ]


def first_call(xs, gains, w_mine, w_other):
    pieces = len(xs)
    rows, width = xs[0].shape
    total, cols = rows * pieces, w_mine.shape[2]
    return pl.pallas_call(
        functools.partial(first_kernel, pieces),
        in_specs=[VMEM] * (pieces + 2) + [ANY, ANY],
        out_specs=[VMEM] * 3,
        out_shape=qkv_shapes(total, cols) + [pltpu.VMEM((6, width, cols), jnp.bfloat16)],
        scratch_shapes=[pltpu.VMEM((total, width), jnp.bfloat16), pltpu.SemaphoreType.DMA((6,))],
        compiler_params=pltpu.CompilerParams(vmem_limit_bytes=24 * MIB),
        cost_estimate=pl.CostEstimate(
            flops=40 * 12 * total * width * cols, bytes_accessed=12 * width * cols, transcendentals=0
        ),
    )(
        *xs,
        *gains,
        pltpu.with_memory_space_constraint(w_mine, pltpu.HBM),
        w_other,
    )


def rest_call(xs, gains, held):
    pieces = len(xs)
    rows, width = xs[0].shape
    total, cols = rows * pieces, held.shape[2]
    return pl.pallas_call(
        functools.partial(rest_kernel, pieces),
        in_specs=[VMEM] * (pieces + 3),
        out_specs=[VMEM] * 2,
        out_shape=qkv_shapes(total, cols),
        scratch_shapes=[pltpu.VMEM((total, width), jnp.bfloat16)],
        compiler_params=pltpu.CompilerParams(vmem_limit_bytes=24 * MIB),
        cost_estimate=pl.CostEstimate(
            flops=12 * total * width * cols, bytes_accessed=12 * width * cols, transcendentals=0
        ),
    )(*xs, *gains, pltpu.with_memory_space_constraint(held, pltpu.VMEM))


def attend(q_ref, kv_ref, attn_ref):
    cols = q_ref.shape[2]
    contract = (((1,), (1,)), ((), ()))
    for owner in range(2):
        for at in range(0, cols, HEAD_DIM):
            span = slice(at, at + HEAD_DIM)
            scores = lax.dot_general(
                q_ref[owner, :, span], kv_ref[2 * owner, :, span], contract, preferred_element_type=jnp.float32
            ) * HEAD_DIM ** (-0.5)
            top = jnp.max(scores, axis=-1, keepdims=True)
            expo = jnp.exp(scores - top)
            total = jnp.sum(expo, axis=-1, keepdims=True)
            prob = (expo * (1.0 / total)).astype(jnp.bfloat16)
            value = jnp.dot(prob, kv_ref[2 * owner + 1, :, span], preferred_element_type=jnp.float32)
            attn_ref[:, owner * cols + at : owner * cols + at + HEAD_DIM] = value.astype(jnp.bfloat16)


def out_project(attn_ref, w_mine, w_other, outs):
    rows, cols = outs[0].shape[0], w_mine.shape[0]
    part = jnp.dot(attn_ref[:, :cols], w_mine[...], preferred_element_type=jnp.float32)
    part += jnp.dot(attn_ref[:, cols:], w_other[...], preferred_element_type=jnp.float32)
    part = part.astype(jnp.bfloat16)
    for i, out in enumerate(outs):
        out[...] = part[i * rows : (i + 1) * rows, :]


def far_kernel(pieces, q_a, q_b, kv_a, kv_b, far_a, far_b, w_mine, w_other, *refs):
    outs, (kv_ref, q_ref, attn_ref) = refs[:pieces], refs[pieces:]

    @pl.when(pl.program_id(0) == 0)
    def _():
        cut, most = q_a.shape[1], q_b.shape[1]
        half, tail = cut + most, q_ref.shape[1] - most
        for owner in range(2):
            q_ref[owner, :most, :] = q_b[owner]
            q_ref[owner, most:, :] = q_a[owner, cut - tail :, :]
            for kind in range(2):
                near, far = 2 * owner + kind, 2 * (1 - owner) + kind
                kv_ref[near, :cut, :] = kv_a[near]
                kv_ref[near, cut:half, :] = kv_b[near]
                kv_ref[near, half : half + cut, :] = far_a[far]
                kv_ref[near, half + cut :, :] = far_b[far]
        attend(q_ref, kv_ref, attn_ref)

    out_project(attn_ref, w_mine, w_other, outs)


def near_kernel(pieces, q_a, kv_ref, w_mine, w_other, *refs):
    outs, (q_ref, attn_ref) = refs[:pieces], refs[pieces:]

    @pl.when(pl.program_id(0) == 0)
    def _():
        q_ref[...] = q_a[:, : q_ref.shape[1], :]
        attend(q_ref, kv_ref, attn_ref)

    out_project(attn_ref, w_mine, w_other, outs)


def attend_call(kernel, operands, w_mine, w_other, rows, pieces, keys=None):
    cols, width = w_mine.shape
    total, block = rows * pieces, 1024
    whole = lambda shape: pl.BlockSpec(shape, lambda i: (0,) * len(shape))
    length = 2 * 8 * rows
    out_shape = [jax.ShapeDtypeStruct((rows, width), jnp.bfloat16)] * pieces
    out_specs = [pl.BlockSpec((rows, block), lambda i: (0, i))] * pieces
    if keys is not None:
        out_shape = out_shape + [jax.ShapeDtypeStruct(keys, jnp.bfloat16)]
        out_specs = out_specs + [whole(keys)]
    return pl.pallas_call(
        functools.partial(kernel, pieces),
        grid=(width // block,),
        in_specs=[whole(x.shape) for x in operands] + [pl.BlockSpec((cols, block), lambda i: (0, i))] * 2,
        out_specs=out_specs,
        out_shape=out_shape,
        scratch_shapes=[
            pltpu.VMEM((2, total, cols), jnp.bfloat16),
            pltpu.VMEM((total, 2 * cols), jnp.bfloat16),
        ],
        compiler_params=pltpu.CompilerParams(vmem_limit_bytes=24 * MIB),
        cost_estimate=pl.CostEstimate(
            flops=4 * total * cols * width + 8 * total * length * cols,
            bytes_accessed=4 * cols * width,
            transcendentals=4 * total * length,
        ),
    )(*operands, w_mine, w_other)


def body(latents, steps, leaving, fresh, mod_table, w_qkv, q_gain, k_gain, w_out):
    _, frames, local_rows, width = latents.shape
    rows = frames * local_rows
    own = latents.reshape(rows, width)
    normed, gate, gain = norm_call(steps, own, mod_table, q_gain[None], k_gain[None])

    w_mine = w_qkv.transpose(1, 0, 2)
    gains = [gain, hop(gain, dc=1)]
    w_send, _ = lax.optimization_barrier((w_mine, gains[1]))
    w_other = hop(w_send, dc=1)

    left = hop(normed, dx=1)
    right = hop(normed, dx=-1)
    far = hop(normed, dz=1)
    across = hop(normed, dx=2)
    far_left = hop(left, dz=1)
    right_send, out_send, _ = lax.optimization_barrier((right, w_out, w_other))
    far_right = hop(right_send, dz=1)
    far_across = hop(far, dx=2)

    out_other = hop(out_send, dc=1)

    q_a, kv_a, held = first_call([normed, left, right, far, across], gains, w_mine, w_other)
    far_a = hop(kv_a, dc=1)
    q_b, kv_b = rest_call([far_left, far_right, far_across], gains, held)
    far_b = hop(kv_b, dc=1)
    keys = (4, 16 * rows, kv_a.shape[2])
    operands = (q_a, q_b, kv_a, kv_b, far_a, far_b)
    p_far_left, p_far_right, p_far_across, p_across, kv = attend_call(
        far_kernel, operands, w_out, out_other, rows, 4, keys
    )
    p_own, p_left, p_right, p_far = attend_call(near_kernel, (q_a, kv), w_out, out_other, rows, 4)

    def add(a, b):
        return (a.astype(jnp.float32) + b.astype(jnp.float32)).astype(jnp.bfloat16)

    s_left = add(p_left, hop(p_far_left, dz=1))
    s_right = add(p_right, hop(p_far_right, dz=1))
    s_far = add(p_far, hop(p_far_across, dx=2))
    arrived = [hop(p_across, dx=2), hop(s_left, dx=-1), hop(s_right, dx=1), hop(s_far, dz=1)]
    proj = p_own.astype(jnp.float32)
    for piece in arrived:
        proj = proj + piece.astype(jnp.float32)

    updated = (own.astype(jnp.float32) + gate * proj).astype(jnp.bfloat16).reshape(frames, local_rows, width)
    handed = lax.dynamic_slice_in_dim(updated, leaving[0], 1, axis=0)[0]
    arriving = from_behind(handed, "queue", 1)
    first = jnp.where(lax.axis_index("queue") == 0, fresh, arriving)
    select = jnp.arange(frames) == leaving[0]
    return jnp.where(select[:, None, None], first[None], updated)[None]


def solution(mesh):
    return jax.shard_map(
        body,
        mesh=mesh,
        in_specs=(
            P("queue", None, "seq", None),
            P("queue"),
            P("queue"),
            P("seq", None),
            P(),
            P(None, None, "seq"),
            P("seq"),
            P("seq"),
            P("seq", None),
        ),
        out_specs=P("queue", None, "seq", None),
        check_vma=False,
    )
```

```python
import functools

import jax
import jax.numpy as jnp
from jax import lax
from jax.experimental import pallas as pl
from jax.experimental.pallas import tpu as pltpu
from jax.sharding import PartitionSpec as P

HEAD_DIM = 128
Z_CHIPS, X_CHIPS, CORES = 2, 4, 2
MIB = 1 << 20
ANY = pl.BlockSpec(memory_space=pl.ANY)
VMEM = pl.BlockSpec(memory_space=pltpu.VMEM)
SMEM = pl.BlockSpec(memory_space=pltpu.SMEM)


def hop(value, dz=0, dx=0, dc=0):
    pairs = []
    for z in range(Z_CHIPS):
        for x in range(X_CHIPS):
            for c in range(CORES):
                to_z, to_x, to_c = (z + dz) % Z_CHIPS, (x + dx) % X_CHIPS, (c + dc) % CORES
                pairs.append(((z * X_CHIPS + x) * CORES + c, (to_z * X_CHIPS + to_x) * CORES + to_c))
    return lax.ppermute(value, "seq", pairs)


def from_behind(x, axis, by):
    count = lax.axis_size(axis)
    pairs = [(i, i + by) for i in range(count) if 0 <= i + by < count]
    return lax.ppermute(x, axis, pairs)


def norm_kernel(step, x_hbm, table, q_hbm, k_hbm, out_ref, gate_ref, gain_ref, x_ref, row, q_ref, k_ref, sems):
    width = x_hbm.shape[-1]
    moves = [(x_hbm, x_ref), (table.at[pl.ds(step[0], 1), :], row), (q_hbm, q_ref), (k_hbm, k_ref)]
    copies = [pltpu.make_async_copy(src, dst, sems.at[i]) for i, (src, dst) in enumerate(moves)]
    for copy in copies:
        copy.start()
    copies[0].wait()
    values = x_ref[...].astype(jnp.float32)
    mean = jnp.mean(values, axis=-1, keepdims=True)
    centred = values - mean
    var = jnp.mean(centred * centred, axis=-1, keepdims=True)
    scaled = centred * lax.rsqrt(var + 1e-06)
    for copy in copies[1:]:
        copy.wait()
    shift, scale = row[:, :width], row[:, width : 2 * width]
    out_ref[...] = (scaled * (1.0 + scale) + shift).astype(jnp.bfloat16)
    gate_ref[...] = row[:, 2 * width :]
    gain_ref[0:1, :] = q_ref[...]
    gain_ref[1:2, :] = k_ref[...]


def norm_call(step, x, table, q_gain, k_gain):
    rows, width = x.shape
    cols = q_gain.shape[1]
    in_hbm = lambda array: pltpu.with_memory_space_constraint(array, pltpu.HBM)
    return pl.pallas_call(
        norm_kernel,
        in_specs=[SMEM] + [ANY] * 4,
        out_specs=[VMEM] * 3,
        out_shape=[
            jax.ShapeDtypeStruct((rows, width), jnp.bfloat16),
            jax.ShapeDtypeStruct((1, width), jnp.float32),
            jax.ShapeDtypeStruct((2, cols), jnp.float32),
        ],
        scratch_shapes=[
            pltpu.VMEM((rows, width), jnp.bfloat16),
            pltpu.VMEM((1, 3 * width), jnp.float32),
            pltpu.VMEM((1, cols), jnp.float32),
            pltpu.VMEM((1, cols), jnp.float32),
            pltpu.SemaphoreType.DMA((4,)),
        ],
        compiler_params=pltpu.CompilerParams(vmem_limit_bytes=8 * MIB),
        cost_estimate=pl.CostEstimate(flops=10 * rows * width, bytes_accessed=4 * rows * width, transcendentals=0),
    )(step, in_hbm(x), in_hbm(table), in_hbm(q_gain), in_hbm(k_gain))


def head_norm(values, gain):
    out = []
    for at in range(0, values.shape[1], HEAD_DIM):
        part = values[:, at : at + HEAD_DIM]
        power = jnp.mean(part * part, axis=-1, keepdims=True)
        out.append(part * lax.rsqrt(power + 1e-06) * gain[:, at : at + HEAD_DIM])
    return jnp.concatenate(out, axis=1)


def project(i, rows_ref, weights, gains, q_ref, kv_ref):
    owner, kind = divmod(i, 3)
    acc = jnp.dot(rows_ref[...], weights[owner][kind], preferred_element_type=jnp.float32)
    if kind < 2:
        gain = gains[1 + kind][...] if owner else gains[0][kind : kind + 1, :]
        acc = head_norm(acc, gain)
    if kind == 0:
        q_ref[owner] = acc.astype(jnp.bfloat16)
    else:
        kv_ref[2 * owner + kind - 1] = acc.astype(jnp.bfloat16)


def gather_rows(xs, rows_ref):
    rows = xs[0].shape[0]
    for i, x in enumerate(xs):
        rows_ref[i * rows : (i + 1) * rows, :] = x[...]


def first_kernel(pieces, *refs):
    xs, gains = refs[:pieces], refs[pieces : pieces + 3]
    w_mine, w_other, q_ref, kv_ref, held, rows_ref, sems = refs[pieces + 3 :]
    copies = []
    for i in range(3):
        copies.append(pltpu.make_async_copy(w_mine.at[i], held.at[i], sems.at[i]))
        copies[i].start()
    gather_rows(xs, rows_ref)
    for i in (3, 4, 5, 0, 1, 2):
        if i < 3:
            copies[i].wait()
        project(i, rows_ref, (held, w_other), gains, q_ref, kv_ref)


def rest_kernel(pieces, *refs):
    xs, gains = refs[:pieces], refs[pieces : pieces + 3]
    held, w_other, q_ref, kv_ref, rows_ref = refs[pieces + 3 :]
    gather_rows(xs, rows_ref)
    for i in range(6):
        project(i, rows_ref, (held, w_other), gains, q_ref, kv_ref)


def qkv_shapes(total, cols):
    return [
        jax.ShapeDtypeStruct((2, total, cols), jnp.bfloat16),
        jax.ShapeDtypeStruct((4, total, cols), jnp.bfloat16),
    ]


def first_call(xs, gains, w_mine, w_other):
    pieces = len(xs)
    rows, width = xs[0].shape
    total, cols = rows * pieces, w_mine.shape[2]
    return pl.pallas_call(
        functools.partial(first_kernel, pieces),
        in_specs=[VMEM] * (pieces + 3) + [ANY, VMEM],
        out_specs=[VMEM] * 3,
        out_shape=qkv_shapes(total, cols) + [pltpu.VMEM((3, width, cols), jnp.bfloat16)],
        scratch_shapes=[pltpu.VMEM((total, width), jnp.bfloat16), pltpu.SemaphoreType.DMA((3,))],
        compiler_params=pltpu.CompilerParams(vmem_limit_bytes=24 * MIB),
        cost_estimate=pl.CostEstimate(
            flops=40 * 12 * total * width * cols, bytes_accessed=12 * width * cols, transcendentals=0
        ),
    )(
        *xs,
        *gains,
        pltpu.with_memory_space_constraint(w_mine, pltpu.HBM),
        pltpu.with_memory_space_constraint(w_other, pltpu.VMEM),
    )


def rest_call(xs, gains, held, w_other):
    pieces = len(xs)
    rows, width = xs[0].shape
    total, cols = rows * pieces, held.shape[2]
    return pl.pallas_call(
        functools.partial(rest_kernel, pieces),
        in_specs=[VMEM] * (pieces + 5),
        out_specs=[VMEM] * 2,
        out_shape=qkv_shapes(total, cols),
        scratch_shapes=[pltpu.VMEM((total, width), jnp.bfloat16)],
        compiler_params=pltpu.CompilerParams(vmem_limit_bytes=24 * MIB),
        cost_estimate=pl.CostEstimate(
            flops=12 * total * width * cols, bytes_accessed=12 * width * cols, transcendentals=0
        ),
    )(
        *xs,
        *gains,
        pltpu.with_memory_space_constraint(held, pltpu.VMEM),
        pltpu.with_memory_space_constraint(w_other, pltpu.VMEM),
    )


def attend(q_ref, kv_ref, attn_ref):
    cols = q_ref.shape[2]
    contract = (((1,), (1,)), ((), ()))
    for owner in range(2):
        for at in range(0, cols, HEAD_DIM):
            span = slice(at, at + HEAD_DIM)
            scores = lax.dot_general(
                q_ref[owner, :, span], kv_ref[2 * owner, :, span], contract, preferred_element_type=jnp.float32
            ) * HEAD_DIM ** (-0.5)
            top = jnp.max(scores, axis=-1, keepdims=True)
            expo = jnp.exp(scores - top)
            total = jnp.sum(expo, axis=-1, keepdims=True)
            prob = (expo * (1.0 / total)).astype(jnp.bfloat16)
            value = jnp.dot(prob, kv_ref[2 * owner + 1, :, span], preferred_element_type=jnp.float32)
            attn_ref[:, owner * cols + at : owner * cols + at + HEAD_DIM] = value.astype(jnp.bfloat16)


def out_project(attn_ref, w_mine, w_other, outs):
    rows, cols = outs[0].shape[0], w_mine.shape[0]
    part = jnp.dot(attn_ref[:, :cols], w_mine[...], preferred_element_type=jnp.float32)
    part += jnp.dot(attn_ref[:, cols:], w_other[...], preferred_element_type=jnp.float32)
    part = part.astype(jnp.bfloat16)
    for i, out in enumerate(outs):
        out[...] = part[i * rows : (i + 1) * rows, :]


def far_kernel(pieces, q_a, q_b, kv_a, kv_b, far_a, far_b, w_mine, w_other, *refs):
    outs, (kv_ref, q_ref, attn_ref) = refs[:pieces], refs[pieces:]

    @pl.when(pl.program_id(0) == 0)
    def _():
        cut, most = q_a.shape[1], q_b.shape[1]
        half, tail = cut + most, q_ref.shape[1] - most
        for owner in range(2):
            q_ref[owner, :most, :] = q_b[owner]
            q_ref[owner, most:, :] = q_a[owner, cut - tail :, :]
            for kind in range(2):
                near, far = 2 * owner + kind, 2 * (1 - owner) + kind
                kv_ref[near, :cut, :] = kv_a[near]
                kv_ref[near, cut:half, :] = kv_b[near]
                kv_ref[near, half : half + cut, :] = far_a[far]
                kv_ref[near, half + cut :, :] = far_b[far]
        attend(q_ref, kv_ref, attn_ref)

    out_project(attn_ref, w_mine, w_other, outs)


def near_kernel(pieces, q_a, kv_ref, w_mine, w_other, *refs):
    outs, (q_ref, attn_ref) = refs[:pieces], refs[pieces:]

    @pl.when(pl.program_id(0) == 0)
    def _():
        q_ref[...] = q_a[:, : q_ref.shape[1], :]
        attend(q_ref, kv_ref, attn_ref)

    out_project(attn_ref, w_mine, w_other, outs)


def attend_call(kernel, operands, w_mine, w_other, rows, pieces, keys=None):
    cols, width = w_mine.shape
    total, block = rows * pieces, 1024
    whole = lambda shape: pl.BlockSpec(shape, lambda i: (0,) * len(shape))
    length = 2 * 8 * rows
    out_shape = [jax.ShapeDtypeStruct((rows, width), jnp.bfloat16)] * pieces
    out_specs = [pl.BlockSpec((rows, block), lambda i: (0, i))] * pieces
    if keys is not None:
        out_shape = out_shape + [jax.ShapeDtypeStruct(keys, jnp.bfloat16)]
        out_specs = out_specs + [whole(keys)]
    return pl.pallas_call(
        functools.partial(kernel, pieces),
        grid=(width // block,),
        in_specs=[whole(x.shape) for x in operands] + [pl.BlockSpec((cols, block), lambda i: (0, i))] * 2,
        out_specs=out_specs,
        out_shape=out_shape,
        scratch_shapes=[
            pltpu.VMEM((2, total, cols), jnp.bfloat16),
            pltpu.VMEM((total, 2 * cols), jnp.bfloat16),
        ],
        compiler_params=pltpu.CompilerParams(vmem_limit_bytes=24 * MIB),
        cost_estimate=pl.CostEstimate(
            flops=4 * total * cols * width + 8 * total * length * cols,
            bytes_accessed=4 * cols * width,
            transcendentals=4 * total * length,
        ),
    )(*operands, w_mine, w_other)


def body(latents, steps, leaving, fresh, mod_table, w_qkv, q_gain, k_gain, w_out):
    _, frames, local_rows, width = latents.shape
    rows = frames * local_rows
    own = latents.reshape(rows, width)
    normed, gate, gain = norm_call(steps, own, mod_table, q_gain[None], k_gain[None])

    w_mine = w_qkv.transpose(1, 0, 2)
    q_other, k_other = hop(q_gain[None], dc=1), hop(k_gain[None], dc=1)
    gains = [gain, q_other, k_other]
    w_send, _, _, _ = lax.optimization_barrier((w_mine, q_other, k_other, normed))
    w_other = hop(w_send, dc=1)

    left = hop(normed, dx=1)
    right = hop(normed, dx=-1)
    far = hop(normed, dz=1)
    across_send, _ = lax.optimization_barrier((normed, left))
    across = hop(across_send, dx=2)
    far_left = hop(left, dz=1)
    far_right = hop(right, dz=1)
    far_send, out_send, _ = lax.optimization_barrier((far, w_out, w_other))
    far_across = hop(far_send, dx=2)

    out_other = hop(out_send, dc=1)

    q_a, kv_a, held = first_call([normed, left, right, far, across], gains, w_mine, w_other)
    far_a = hop(kv_a, dc=1)
    q_b, kv_b = rest_call([far_left, far_right, far_across], gains, held, w_other)
    far_b = hop(kv_b, dc=1)
    keys = (4, 16 * rows, kv_a.shape[2])
    operands = (q_a, q_b, kv_a, kv_b, far_a, far_b)
    p_far_left, p_far_right, p_far_across, p_across, kv = attend_call(
        far_kernel, operands, w_out, out_other, rows, 4, keys
    )
    p_own, p_left, p_right, p_far = attend_call(near_kernel, (q_a, kv), w_out, out_other, rows, 4)

    def add(a, b):
        return (a.astype(jnp.float32) + b.astype(jnp.float32)).astype(jnp.bfloat16)

    from_across = hop(p_far_across, dx=2)
    across_send, _ = lax.optimization_barrier((p_across, from_across))
    s_left = add(p_left, hop(p_far_left, dz=1))
    s_right = add(p_right, hop(p_far_right, dz=1))
    s_far = add(p_far, from_across)
    arrived = [hop(across_send, dx=2), hop(s_left, dx=-1), hop(s_right, dx=1), hop(s_far, dz=1)]
    proj = p_own.astype(jnp.float32)
    for piece in arrived:
        proj = proj + piece.astype(jnp.float32)

    updated = (own.astype(jnp.float32) + gate * proj).astype(jnp.bfloat16).reshape(frames, local_rows, width)
    handed = lax.dynamic_slice_in_dim(updated, leaving[0], 1, axis=0)[0]
    arriving = from_behind(handed, "queue", 1)
    first = jnp.where(lax.axis_index("queue") == 0, fresh, arriving)
    select = jnp.arange(frames) == leaving[0]
    return jnp.where(select[:, None, None], first[None], updated)[None]


def solution(mesh):
    return jax.shard_map(
        body,
        mesh=mesh,
        in_specs=(
            P("queue", None, "seq", None),
            P("queue"),
            P("queue"),
            P("seq", None),
            P(),
            P(None, None, "seq"),
            P("seq"),
            P("seq"),
            P("seq", None),
        ),
        out_specs=P("queue", None, "seq", None),
        check_vma=False,
    )
```

```python
import functools

import jax
import jax.numpy as jnp
from jax import lax
from jax.experimental import pallas as pl
from jax.experimental.pallas import tpu as pltpu
from jax.sharding import PartitionSpec as P

HEAD_DIM = 128
Z_CHIPS, X_CHIPS, CORES = 2, 4, 2
MIB = 1 << 20
ANY = pl.BlockSpec(memory_space=pl.ANY)
VMEM = pl.BlockSpec(memory_space=pltpu.VMEM)
SMEM = pl.BlockSpec(memory_space=pltpu.SMEM)


def hop(value, dz=0, dx=0, dc=0):
    pairs = []
    for z in range(Z_CHIPS):
        for x in range(X_CHIPS):
            for c in range(CORES):
                to_z, to_x, to_c = (z + dz) % Z_CHIPS, (x + dx) % X_CHIPS, (c + dc) % CORES
                pairs.append(((z * X_CHIPS + x) * CORES + c, (to_z * X_CHIPS + to_x) * CORES + to_c))
    return lax.ppermute(value, "seq", pairs)


def from_behind(x, axis, by):
    count = lax.axis_size(axis)
    pairs = [(i, (i + by) % count) for i in range(count)]
    return lax.ppermute(x, axis, pairs)


def norm_kernel(step, x_hbm, table, q_hbm, k_hbm, out_ref, gate_ref, gain_ref, x_ref, row, q_ref, k_ref, sems):
    width = x_hbm.shape[-1]
    moves = [(x_hbm, x_ref), (table.at[pl.ds(step[0], 1), :], row), (q_hbm, q_ref), (k_hbm, k_ref)]
    copies = [pltpu.make_async_copy(src, dst, sems.at[i]) for i, (src, dst) in enumerate(moves)]
    for copy in copies:
        copy.start()
    copies[0].wait()
    values = x_ref[...].astype(jnp.float32)
    mean = jnp.mean(values, axis=-1, keepdims=True)
    centred = values - mean
    var = jnp.mean(centred * centred, axis=-1, keepdims=True)
    scaled = centred * lax.rsqrt(var + 1e-06)
    for copy in copies[1:]:
        copy.wait()
    shift, scale = row[:, :width], row[:, width : 2 * width]
    out_ref[...] = (scaled * (1.0 + scale) + shift).astype(jnp.bfloat16)
    gate_ref[...] = row[:, 2 * width :]
    gain_ref[0:1, :] = q_ref[...]
    gain_ref[1:2, :] = k_ref[...]


def norm_call(step, x, table, q_gain, k_gain):
    rows, width = x.shape
    cols = q_gain.shape[1]
    in_hbm = lambda array: pltpu.with_memory_space_constraint(array, pltpu.HBM)
    return pl.pallas_call(
        norm_kernel,
        in_specs=[SMEM] + [ANY] * 4,
        out_specs=[VMEM] * 3,
        out_shape=[
            jax.ShapeDtypeStruct((rows, width), jnp.bfloat16),
            jax.ShapeDtypeStruct((1, width), jnp.float32),
            jax.ShapeDtypeStruct((2, cols), jnp.float32),
        ],
        scratch_shapes=[
            pltpu.VMEM((rows, width), jnp.bfloat16),
            pltpu.VMEM((1, 3 * width), jnp.float32),
            pltpu.VMEM((1, cols), jnp.float32),
            pltpu.VMEM((1, cols), jnp.float32),
            pltpu.SemaphoreType.DMA((4,)),
        ],
        compiler_params=pltpu.CompilerParams(vmem_limit_bytes=8 * MIB),
        cost_estimate=pl.CostEstimate(flops=10 * rows * width, bytes_accessed=4 * rows * width, transcendentals=0),
    )(step, in_hbm(x), in_hbm(table), in_hbm(q_gain), in_hbm(k_gain))


def head_norm(values, gain):
    out = []
    for at in range(0, values.shape[1], HEAD_DIM):
        part = values[:, at : at + HEAD_DIM]
        power = jnp.mean(part * part, axis=-1, keepdims=True)
        out.append(part * lax.rsqrt(power + 1e-06) * gain[:, at : at + HEAD_DIM])
    return jnp.concatenate(out, axis=1)


def project(i, rows_ref, weights, gains, q_ref, kv_ref):
    owner, kind = divmod(i, 3)
    acc = jnp.dot(rows_ref[...], weights[owner][kind], preferred_element_type=jnp.float32)
    if kind < 2:
        gain = gains[1 + kind][...] if owner else gains[0][kind : kind + 1, :]
        acc = head_norm(acc, gain)
    if kind == 0:
        q_ref[owner] = acc.astype(jnp.bfloat16)
    else:
        kv_ref[2 * owner + kind - 1] = acc.astype(jnp.bfloat16)


def gather_rows(xs, rows_ref):
    at = 0
    for x in xs:
        rows_ref[at : at + x.shape[0], :] = x[...]
        at += x.shape[0]


def first_kernel(pieces, *refs):
    xs, gains = refs[:pieces], refs[pieces : pieces + 3]
    w_mine, w_other, q_ref, kv_ref, held, rows_ref, sems = refs[pieces + 3 :]
    copies = []
    for i in range(3):
        copies.append(pltpu.make_async_copy(w_mine.at[i], held.at[i], sems.at[i]))
        copies[i].start()
    gather_rows(xs, rows_ref)
    for i in (3, 4, 5, 0, 1, 2):
        if i < 3:
            copies[i].wait()
        project(i, rows_ref, (held, w_other), gains, q_ref, kv_ref)


def rest_kernel(pieces, *refs):
    xs, gains = refs[:pieces], refs[pieces : pieces + 3]
    held, w_other, q_ref, kv_ref, rows_ref = refs[pieces + 3 :]
    gather_rows(xs, rows_ref)
    for i in range(6):
        project(i, rows_ref, (held, w_other), gains, q_ref, kv_ref)


def qkv_shapes(total, cols):
    return [
        jax.ShapeDtypeStruct((2, total, cols), jnp.bfloat16),
        jax.ShapeDtypeStruct((4, total, cols), jnp.bfloat16),
    ]


def first_call(xs, gains, w_mine, w_other):
    pieces = len(xs)
    width = xs[0].shape[1]
    total, cols = sum(x.shape[0] for x in xs), w_mine.shape[2]
    return pl.pallas_call(
        functools.partial(first_kernel, pieces),
        in_specs=[VMEM] * (pieces + 3) + [ANY, VMEM],
        out_specs=[VMEM] * 3,
        out_shape=qkv_shapes(total, cols) + [pltpu.VMEM((3, width, cols), jnp.bfloat16)],
        scratch_shapes=[pltpu.VMEM((total, width), jnp.bfloat16), pltpu.SemaphoreType.DMA((3,))],
        compiler_params=pltpu.CompilerParams(vmem_limit_bytes=24 * MIB),
        cost_estimate=pl.CostEstimate(
            flops=40 * 12 * total * width * cols, bytes_accessed=12 * width * cols, transcendentals=0
        ),
    )(
        *xs,
        *gains,
        pltpu.with_memory_space_constraint(w_mine, pltpu.HBM),
        pltpu.with_memory_space_constraint(w_other, pltpu.VMEM),
    )


def rest_call(xs, gains, held, w_other):
    pieces = len(xs)
    width = xs[0].shape[1]
    total, cols = sum(x.shape[0] for x in xs), held.shape[2]
    return pl.pallas_call(
        functools.partial(rest_kernel, pieces),
        in_specs=[VMEM] * (pieces + 5),
        out_specs=[VMEM] * 2,
        out_shape=qkv_shapes(total, cols),
        scratch_shapes=[pltpu.VMEM((total, width), jnp.bfloat16)],
        compiler_params=pltpu.CompilerParams(vmem_limit_bytes=24 * MIB),
        cost_estimate=pl.CostEstimate(
            flops=12 * total * width * cols, bytes_accessed=12 * width * cols, transcendentals=0
        ),
    )(
        *xs,
        *gains,
        pltpu.with_memory_space_constraint(held, pltpu.VMEM),
        pltpu.with_memory_space_constraint(w_other, pltpu.VMEM),
    )


def attend(q_ref, kv_ref, attn_ref):
    cols = q_ref.shape[2]
    contract = (((1,), (1,)), ((), ()))
    for owner in range(2):
        for at in range(0, cols, HEAD_DIM):
            span = slice(at, at + HEAD_DIM)
            scores = lax.dot_general(
                q_ref[owner, :, span], kv_ref[2 * owner, :, span], contract, preferred_element_type=jnp.float32
            ) * HEAD_DIM ** (-0.5)
            top = jnp.max(scores, axis=-1, keepdims=True)
            expo = jnp.exp(scores - top)
            total = jnp.sum(expo, axis=-1, keepdims=True)
            prob = (expo * (1.0 / total)).astype(jnp.bfloat16)
            value = jnp.dot(prob, kv_ref[2 * owner + 1, :, span], preferred_element_type=jnp.float32)
            attn_ref[:, owner * cols + at : owner * cols + at + HEAD_DIM] = value.astype(jnp.bfloat16)


def out_project(attn_ref, w_mine, w_other, outs):
    cols, at = w_mine.shape[0], 0
    part = jnp.dot(attn_ref[:, :cols], w_mine[...], preferred_element_type=jnp.float32)
    part += jnp.dot(attn_ref[:, cols:], w_other[...], preferred_element_type=jnp.float32)
    part = part.astype(jnp.bfloat16)
    for out in outs:
        out[...] = part[at : at + out.shape[0], :]
        at += out.shape[0]


def far_kernel(pieces, q_a, q_b, kv_a, kv_b, far_a, far_b, w_mine, w_other, *refs):
    outs, (kv_ref, q_ref, attn_ref) = refs[:pieces], refs[pieces:]

    @pl.when(pl.program_id(0) == 0)
    def _():
        cut, most = q_a.shape[1], q_b.shape[1]
        half, tail = cut + most, q_ref.shape[1] - most
        for owner in range(2):
            q_ref[owner, :most, :] = q_b[owner]
            if tail:
                q_ref[owner, most:, :] = q_a[owner, cut - tail :, :]
            for kind in range(2):
                near, far = 2 * owner + kind, 2 * (1 - owner) + kind
                kv_ref[near, :cut, :] = kv_a[near]
                kv_ref[near, cut:half, :] = kv_b[near]
                kv_ref[near, half : half + cut, :] = far_a[far]
                kv_ref[near, half + cut :, :] = far_b[far]
        attend(q_ref, kv_ref, attn_ref)

    out_project(attn_ref, w_mine, w_other, outs)


def near_kernel(pieces, q_a, kv_ref, w_mine, w_other, *refs):
    outs, (q_ref, attn_ref) = refs[:pieces], refs[pieces:]

    @pl.when(pl.program_id(0) == 0)
    def _():
        q_ref[...] = q_a[:, : q_ref.shape[1], :]
        attend(q_ref, kv_ref, attn_ref)

    out_project(attn_ref, w_mine, w_other, outs)


def attend_call(kernel, operands, w_mine, w_other, sizes, length, keys=None):
    cols, width = w_mine.shape
    total, block = sum(sizes), 1024
    whole = lambda shape: pl.BlockSpec(shape, lambda i: (0,) * len(shape))
    out_shape = [jax.ShapeDtypeStruct((rows, width), jnp.bfloat16) for rows in sizes]
    out_specs = [pl.BlockSpec((rows, block), lambda i: (0, i)) for rows in sizes]
    if keys is not None:
        out_shape = out_shape + [jax.ShapeDtypeStruct(keys, jnp.bfloat16)]
        out_specs = out_specs + [whole(keys)]
    return pl.pallas_call(
        functools.partial(kernel, len(sizes)),
        grid=(width // block,),
        in_specs=[whole(x.shape) for x in operands] + [pl.BlockSpec((cols, block), lambda i: (0, i))] * 2,
        out_specs=out_specs,
        out_shape=out_shape,
        scratch_shapes=[
            pltpu.VMEM((2, total, cols), jnp.bfloat16),
            pltpu.VMEM((total, 2 * cols), jnp.bfloat16),
        ],
        compiler_params=pltpu.CompilerParams(vmem_limit_bytes=24 * MIB),
        cost_estimate=pl.CostEstimate(
            flops=4 * total * cols * width + 8 * total * length * cols,
            bytes_accessed=4 * cols * width,
            transcendentals=4 * total * length,
        ),
    )(*operands, w_mine, w_other)


def body(latents, steps, leaving, fresh, mod_table, w_qkv, q_gain, k_gain, w_out):
    _, frames, local_rows, width = latents.shape
    rows = frames * local_rows
    own = latents.reshape(rows, width)
    normed, gate, gain = norm_call(steps, own, mod_table, q_gain[None], k_gain[None])

    w_mine = w_qkv.transpose(1, 0, 2)
    q_other, k_other = hop(q_gain[None], dc=1), hop(k_gain[None], dc=1)
    gains = [gain, q_other, k_other]
    w_send, _, _, _ = lax.optimization_barrier((w_mine, q_other, k_other, normed))
    w_other = hop(w_send, dc=1)

    left = hop(normed, dx=1)
    right = hop(normed, dx=-1)
    far = hop(normed, dz=1)
    across_send, _ = lax.optimization_barrier((normed, left))
    across = [hop(across_send, dx=2)]
    far_left = hop(left, dz=1)
    far_right = hop(right, dz=1)
    far_send, out_send, _ = lax.optimization_barrier((far, w_out, w_other))
    far_across = hop(far_send, dx=2)

    out_other = hop(out_send, dc=1)

    q_a, kv_a, held = first_call([normed, left, right, far], gains, w_mine, w_other)
    far_a = hop(kv_a, dc=1)
    q_b, kv_b = rest_call([far_left, far_right, far_across, *across], gains, held, w_other)
    far_b = hop(kv_b, dc=1)
    keys = (4, 16 * rows, kv_a.shape[2])
    operands = (q_a, q_b, kv_a, kv_b, far_a, far_b)
    sizes = [rows, rows, rows, rows // 2, rows // 2]
    p_far_left, p_far_right, p_far_across, p_before, p_after, kv = attend_call(
        far_kernel, operands, w_out, out_other, sizes, keys[1], keys
    )
    p_own, p_left, p_right, p_far = attend_call(near_kernel, (q_a, kv), w_out, out_other, [rows] * 4, keys[1])

    def add(a, b):
        return (a.astype(jnp.float32) + b.astype(jnp.float32)).astype(jnp.bfloat16)

    def add_part(a, b, part, at):
        total = a.astype(jnp.float32) + b.astype(jnp.float32)
        part = part.astype(jnp.float32)
        halves = (total[: rows // 2], total[rows // 2 :])
        halves = (halves[0] + part, halves[1]) if at == 0 else (halves[0], halves[1] + part)
        return jnp.concatenate(halves, axis=0).astype(jnp.bfloat16)

    s_right = add_part(p_right, hop(p_far_right, dz=1), hop(p_before, dx=1), 0)
    s_left = add_part(p_left, hop(p_far_left, dz=1), hop(p_after, dx=-1), 1)
    s_far = add(p_far, hop(p_far_across, dx=2))
    arrived = [hop(s_left, dx=-1), hop(s_right, dx=1), hop(s_far, dz=1)]
    proj = p_own.astype(jnp.float32)
    for piece in arrived:
        proj = proj + piece.astype(jnp.float32)

    updated = (own.astype(jnp.float32) + gate * proj).astype(jnp.bfloat16).reshape(frames, local_rows, width)
    handed = lax.dynamic_slice_in_dim(updated, leaving[0], 1, axis=0)[0]
    arriving = from_behind(handed, "queue", 1)
    first = jnp.where(lax.axis_index("queue") == 0, fresh, arriving)
    select = jnp.arange(frames) == leaving[0]
    return jnp.where(select[:, None, None], first[None], updated)[None]


def solution(mesh):
    return jax.shard_map(
        body,
        mesh=mesh,
        in_specs=(
            P("queue", None, "seq", None),
            P("queue"),
            P("queue"),
            P("seq", None),
            P(),
            P(None, None, "seq"),
            P("seq"),
            P("seq"),
            P("seq", None),
        ),
        out_specs=P("queue", None, "seq", None),
        check_vma=False,
    )
```

```python
import functools

import jax
import jax.numpy as jnp
from jax import lax
from jax.experimental import pallas as pl
from jax.experimental.pallas import tpu as pltpu
from jax.sharding import PartitionSpec as P

HEAD_DIM = 128
Z_CHIPS, X_CHIPS, CORES = 2, 4, 2
MIB = 1 << 20
ANY = pl.BlockSpec(memory_space=pl.ANY)
VMEM = pl.BlockSpec(memory_space=pltpu.VMEM)
SMEM = pl.BlockSpec(memory_space=pltpu.SMEM)


def hop(value, dz=0, dx=0, dc=0):
    pairs = []
    for z in range(Z_CHIPS):
        for x in range(X_CHIPS):
            for c in range(CORES):
                to_z, to_x, to_c = (z + dz) % Z_CHIPS, (x + dx) % X_CHIPS, (c + dc) % CORES
                pairs.append(((z * X_CHIPS + x) * CORES + c, (to_z * X_CHIPS + to_x) * CORES + to_c))
    return lax.ppermute(value, "seq", pairs)


def from_behind(x, axis, by):
    count = lax.axis_size(axis)
    pairs = [(i, (i + by) % count) for i in range(count)]
    return lax.ppermute(x, axis, pairs)


def norm_kernel(step, x_hbm, table, q_hbm, k_hbm, out_ref, gate_ref, gain_ref, x_ref, row, q_ref, k_ref, sems):
    width = x_hbm.shape[-1]
    moves = [(x_hbm, x_ref), (table.at[pl.ds(step[0], 1), :], row), (q_hbm, q_ref), (k_hbm, k_ref)]
    copies = [pltpu.make_async_copy(src, dst, sems.at[i]) for i, (src, dst) in enumerate(moves)]
    for copy in copies:
        copy.start()
    copies[0].wait()
    values = x_ref[...].astype(jnp.float32)
    mean = jnp.mean(values, axis=-1, keepdims=True)
    centred = values - mean
    var = jnp.mean(centred * centred, axis=-1, keepdims=True)
    scaled = centred * lax.rsqrt(var + 1e-06)
    for copy in copies[1:]:
        copy.wait()
    shift, scale = row[:, :width], row[:, width : 2 * width]
    out_ref[...] = (scaled * (1.0 + scale) + shift).astype(jnp.bfloat16)
    gate_ref[...] = row[:, 2 * width :]
    gain_ref[0:1, :] = q_ref[...]
    gain_ref[1:2, :] = k_ref[...]


def norm_call(step, x, table, q_gain, k_gain):
    rows, width = x.shape
    cols = q_gain.shape[1]
    in_hbm = lambda array: pltpu.with_memory_space_constraint(array, pltpu.HBM)
    return pl.pallas_call(
        norm_kernel,
        in_specs=[SMEM] + [ANY] * 4,
        out_specs=[VMEM] * 3,
        out_shape=[
            jax.ShapeDtypeStruct((rows, width), jnp.bfloat16),
            jax.ShapeDtypeStruct((1, width), jnp.float32),
            jax.ShapeDtypeStruct((2, cols), jnp.float32),
        ],
        scratch_shapes=[
            pltpu.VMEM((rows, width), jnp.bfloat16),
            pltpu.VMEM((1, 3 * width), jnp.float32),
            pltpu.VMEM((1, cols), jnp.float32),
            pltpu.VMEM((1, cols), jnp.float32),
            pltpu.SemaphoreType.DMA((4,)),
        ],
        compiler_params=pltpu.CompilerParams(vmem_limit_bytes=8 * MIB),
        cost_estimate=pl.CostEstimate(flops=10 * rows * width, bytes_accessed=4 * rows * width, transcendentals=0),
    )(step, in_hbm(x), in_hbm(table), in_hbm(q_gain), in_hbm(k_gain))


def head_norm(values, gain):
    out = []
    for at in range(0, values.shape[1], HEAD_DIM):
        part = values[:, at : at + HEAD_DIM]
        power = jnp.mean(part * part, axis=-1, keepdims=True)
        out.append(part * lax.rsqrt(power + 1e-06) * gain[:, at : at + HEAD_DIM])
    return jnp.concatenate(out, axis=1)


def project(i, rows_ref, weights, gains, q_ref, kv_ref):
    owner, kind = divmod(i, 3)
    acc = jnp.dot(rows_ref[...], weights[owner][kind], preferred_element_type=jnp.float32)
    if kind < 2:
        gain = gains[1 + kind][...] if owner else gains[0][kind : kind + 1, :]
        acc = head_norm(acc, gain)
    if kind == 0:
        q_ref[owner] = acc.astype(jnp.bfloat16)
    else:
        kv_ref[2 * owner + kind - 1] = acc.astype(jnp.bfloat16)


def gather_rows(xs, rows_ref):
    at = 0
    for x in xs:
        rows_ref[at : at + x.shape[0], :] = x[...]
        at += x.shape[0]


def first_kernel(pieces, *refs):
    xs, gains = refs[:pieces], refs[pieces : pieces + 3]
    w_mine, w_other, q_ref, kv_ref, held, rows_ref, sems = refs[pieces + 3 :]
    copies = []
    for i in range(3):
        copies.append(pltpu.make_async_copy(w_mine.at[i], held.at[i], sems.at[i]))
        copies[i].start()
    gather_rows(xs, rows_ref)
    for i in (3, 4, 5, 0, 1, 2):
        if i < 3:
            copies[i].wait()
        project(i, rows_ref, (held, w_other), gains, q_ref, kv_ref)


def rest_kernel(pieces, *refs):
    xs, gains = refs[:pieces], refs[pieces : pieces + 3]
    held, w_other, q_ref, kv_ref, rows_ref = refs[pieces + 3 :]
    gather_rows(xs, rows_ref)
    for i in range(6):
        project(i, rows_ref, (held, w_other), gains, q_ref, kv_ref)


def qkv_shapes(total, cols):
    return [
        jax.ShapeDtypeStruct((2, total, cols), jnp.bfloat16),
        jax.ShapeDtypeStruct((4, total, cols), jnp.bfloat16),
    ]


def first_call(xs, gains, w_mine, w_other):
    pieces = len(xs)
    width = xs[0].shape[1]
    total, cols = sum(x.shape[0] for x in xs), w_mine.shape[2]
    return pl.pallas_call(
        functools.partial(first_kernel, pieces),
        in_specs=[VMEM] * (pieces + 3) + [ANY, VMEM],
        out_specs=[VMEM] * 3,
        out_shape=qkv_shapes(total, cols) + [pltpu.VMEM((3, width, cols), jnp.bfloat16)],
        scratch_shapes=[pltpu.VMEM((total, width), jnp.bfloat16), pltpu.SemaphoreType.DMA((3,))],
        compiler_params=pltpu.CompilerParams(vmem_limit_bytes=24 * MIB),
        cost_estimate=pl.CostEstimate(
            flops=40 * 12 * total * width * cols, bytes_accessed=12 * width * cols, transcendentals=0
        ),
    )(
        *xs,
        *gains,
        pltpu.with_memory_space_constraint(w_mine, pltpu.HBM),
        pltpu.with_memory_space_constraint(w_other, pltpu.VMEM),
    )


def rest_call(xs, gains, held, w_other):
    pieces = len(xs)
    width = xs[0].shape[1]
    total, cols = sum(x.shape[0] for x in xs), held.shape[2]
    return pl.pallas_call(
        functools.partial(rest_kernel, pieces),
        in_specs=[VMEM] * (pieces + 5),
        out_specs=[VMEM] * 2,
        out_shape=qkv_shapes(total, cols),
        scratch_shapes=[pltpu.VMEM((total, width), jnp.bfloat16)],
        compiler_params=pltpu.CompilerParams(vmem_limit_bytes=24 * MIB),
        cost_estimate=pl.CostEstimate(
            flops=12 * total * width * cols, bytes_accessed=12 * width * cols, transcendentals=0
        ),
    )(
        *xs,
        *gains,
        pltpu.with_memory_space_constraint(held, pltpu.VMEM),
        pltpu.with_memory_space_constraint(w_other, pltpu.VMEM),
    )


def attend(q_ref, kv_ref, attn_ref):
    cols = q_ref.shape[2]
    contract = (((1,), (1,)), ((), ()))
    for owner in range(2):
        for at in range(0, cols, HEAD_DIM):
            span = slice(at, at + HEAD_DIM)
            scores = lax.dot_general(
                q_ref[owner, :, span], kv_ref[2 * owner, :, span], contract, preferred_element_type=jnp.float32
            ) * HEAD_DIM ** (-0.5)
            top = jnp.max(scores, axis=-1, keepdims=True)
            expo = jnp.exp(scores - top)
            total = jnp.sum(expo, axis=-1, keepdims=True)
            prob = (expo * (1.0 / total)).astype(jnp.bfloat16)
            value = jnp.dot(prob, kv_ref[2 * owner + 1, :, span], preferred_element_type=jnp.float32)
            attn_ref[:, owner * cols + at : owner * cols + at + HEAD_DIM] = value.astype(jnp.bfloat16)


def out_project(attn_ref, w_mine, w_other, outs):
    cols, width = w_mine.shape
    block = 1024
    for start in range(0, width, block):
        span = slice(start, start + block)
        part = jnp.dot(attn_ref[:, :cols], w_mine[:, span], preferred_element_type=jnp.float32)
        part += jnp.dot(attn_ref[:, cols:], w_other[:, span], preferred_element_type=jnp.float32)
        part = part.astype(jnp.bfloat16)
        at = 0
        for out in outs:
            out[:, span] = part[at : at + out.shape[0], :]
            at += out.shape[0]


def far_kernel(pieces, q_b, kv_a, kv_b, far_a, far_b, w_mine, w_other, *refs):
    outs, (kv_ref, attn_ref) = refs[:pieces], refs[pieces:]
    cut, most = kv_a.shape[1], kv_b.shape[1]
    half = cut + most
    for owner in range(2):
        for kind in range(2):
            near, far = 2 * owner + kind, 2 * (1 - owner) + kind
            kv_ref[near, :cut, :] = kv_a[near]
            kv_ref[near, cut:half, :] = kv_b[near]
            kv_ref[near, half : half + cut, :] = far_a[far]
            kv_ref[near, half + cut :, :] = far_b[far]
    attend(q_b, kv_ref, attn_ref)
    out_project(attn_ref, w_mine, w_other, outs)


def near_kernel(pieces, q_ref, kv_ref, w_mine, w_other, *refs):
    outs, attn_ref = refs[:pieces], refs[pieces]
    attend(q_ref, kv_ref, attn_ref)
    out_project(attn_ref, w_mine, w_other, outs)


def attend_call(kernel, operands, w_mine, w_other, sizes, length, keys=None):
    cols, width = w_mine.shape
    total = sum(sizes)
    out_shape = [jax.ShapeDtypeStruct((rows, width), jnp.bfloat16) for rows in sizes]
    if keys is not None:
        out_shape = out_shape + [jax.ShapeDtypeStruct(keys, jnp.bfloat16)]
    in_vmem = lambda array: pltpu.with_memory_space_constraint(array, pltpu.VMEM)
    return pl.pallas_call(
        functools.partial(kernel, len(sizes)),
        in_specs=[VMEM] * (len(operands) + 2),
        out_specs=[VMEM] * len(out_shape),
        out_shape=out_shape,
        scratch_shapes=[pltpu.VMEM((total, 2 * cols), jnp.bfloat16)],
        compiler_params=pltpu.CompilerParams(vmem_limit_bytes=24 * MIB),
        cost_estimate=pl.CostEstimate(
            flops=4 * total * cols * width + 8 * total * length * cols,
            bytes_accessed=4 * cols * width,
            transcendentals=4 * total * length,
        ),
    )(*operands, in_vmem(w_mine), in_vmem(w_other))


def body(latents, steps, leaving, fresh, mod_table, w_qkv, q_gain, k_gain, w_out):
    _, frames, local_rows, width = latents.shape
    rows = frames * local_rows
    own = latents.reshape(rows, width)
    normed, gate, gain = norm_call(steps, own, mod_table, q_gain[None], k_gain[None])

    w_mine = w_qkv.transpose(1, 0, 2)
    q_other, k_other = hop(q_gain[None], dc=1), hop(k_gain[None], dc=1)
    gains = [gain, q_other, k_other]
    w_send, _, _, _ = lax.optimization_barrier((w_mine, q_other, k_other, normed))
    w_other = hop(w_send, dc=1)

    left = hop(normed, dx=1)
    right = hop(normed, dx=-1)
    far = hop(normed, dz=1)
    across_send, _ = lax.optimization_barrier((normed, left))
    across = [hop(across_send, dx=2)]
    far_left = hop(left, dz=1)
    far_right = hop(right, dz=1)
    far_send, out_send, _ = lax.optimization_barrier((far, w_out, w_other))
    far_across = hop(far_send, dx=2)

    out_other = hop(out_send, dc=1)

    q_a, kv_a, held = first_call([normed, left, right, far], gains, w_mine, w_other)
    far_a = hop(kv_a, dc=1)
    q_b, kv_b = rest_call([far_left, far_right, far_across, *across], gains, held, w_other)
    far_b = hop(kv_b, dc=1)
    keys = (4, 16 * rows, kv_a.shape[2])
    half = rows // 2
    p_far_left, p_far_right, p_far_across, p_before, p_after, kv = attend_call(
        far_kernel, (q_b, kv_a, kv_b, far_a, far_b), w_out, out_other, [rows] * 3 + [half] * 2, keys[1], keys
    )
    p_own, p_left, p_right, p_far = attend_call(near_kernel, (q_a, kv), w_out, out_other, [rows] * 4, keys[1])

    def add(a, b):
        return (a.astype(jnp.float32) + b.astype(jnp.float32)).astype(jnp.bfloat16)

    def add_part(a, b, part, at):
        total = a.astype(jnp.float32) + b.astype(jnp.float32)
        part = part.astype(jnp.float32)
        halves = (total[: rows // 2], total[rows // 2 :])
        halves = (halves[0] + part, halves[1]) if at == 0 else (halves[0], halves[1] + part)
        return jnp.concatenate(halves, axis=0).astype(jnp.bfloat16)

    s_right = add_part(p_right, hop(p_far_right, dz=1), hop(p_before, dx=1), 0)
    s_left = add_part(p_left, hop(p_far_left, dz=1), hop(p_after, dx=-1), 1)
    s_far = add(p_far, hop(p_far_across, dx=2))
    arrived = [hop(s_left, dx=-1), hop(s_right, dx=1), hop(s_far, dz=1)]
    proj = p_own.astype(jnp.float32)
    for piece in arrived:
        proj = proj + piece.astype(jnp.float32)

    updated = (own.astype(jnp.float32) + gate * proj).astype(jnp.bfloat16).reshape(frames, local_rows, width)
    handed = lax.dynamic_slice_in_dim(updated, leaving[0], 1, axis=0)[0]
    arriving = from_behind(handed, "queue", 1)
    first = jnp.where(lax.axis_index("queue") == 0, fresh, arriving)
    select = jnp.arange(frames) == leaving[0]
    return jnp.where(select[:, None, None], first[None], updated)[None]


def solution(mesh):
    return jax.shard_map(
        body,
        mesh=mesh,
        in_specs=(
            P("queue", None, "seq", None),
            P("queue"),
            P("queue"),
            P("seq", None),
            P(),
            P(None, None, "seq"),
            P("seq"),
            P("seq"),
            P("seq", None),
        ),
        out_specs=P("queue", None, "seq", None),
        check_vma=False,
    )
```

```python
import functools

import jax
import jax.numpy as jnp
from jax import lax
from jax.experimental import pallas as pl
from jax.experimental.pallas import tpu as pltpu
from jax.sharding import PartitionSpec as P

HEAD_DIM = 128
Z_CHIPS, X_CHIPS, CORES = 2, 4, 2
MIB = 1 << 20
ANY = pl.BlockSpec(memory_space=pl.ANY)
VMEM = pl.BlockSpec(memory_space=pltpu.VMEM)
SMEM = pl.BlockSpec(memory_space=pltpu.SMEM)


def hop(value, dz=0, dx=0, dc=0):
    pairs = []
    for z in range(Z_CHIPS):
        for x in range(X_CHIPS):
            for c in range(CORES):
                to_z, to_x, to_c = (z + dz) % Z_CHIPS, (x + dx) % X_CHIPS, (c + dc) % CORES
                pairs.append(((z * X_CHIPS + x) * CORES + c, (to_z * X_CHIPS + to_x) * CORES + to_c))
    return lax.ppermute(value, "seq", pairs)


def from_behind(x, axis, by):
    count = lax.axis_size(axis)
    pairs = [(i, (i + by) % count) for i in range(count)]
    return lax.ppermute(x, axis, pairs)


def norm_kernel(step, x_hbm, table, q_hbm, k_hbm, out_ref, gate_ref, gain_ref, x_ref, row, q_ref, k_ref, sems):
    width = x_hbm.shape[-1]
    moves = [(x_hbm, x_ref), (table.at[pl.ds(step[0], 1), :], row), (q_hbm, q_ref), (k_hbm, k_ref)]
    copies = [pltpu.make_async_copy(src, dst, sems.at[i]) for i, (src, dst) in enumerate(moves)]
    for copy in copies:
        copy.start()
    copies[0].wait()
    values = x_ref[...].astype(jnp.float32)
    mean = jnp.mean(values, axis=-1, keepdims=True)
    centred = values - mean
    var = jnp.mean(centred * centred, axis=-1, keepdims=True)
    scaled = centred * lax.rsqrt(var + 1e-06)
    for copy in copies[1:]:
        copy.wait()
    shift, scale = row[:, :width], row[:, width : 2 * width]
    out_ref[...] = (scaled * (1.0 + scale) + shift).astype(jnp.bfloat16)
    gate_ref[...] = row[:, 2 * width :]
    gain_ref[0:1, :] = q_ref[...]
    gain_ref[1:2, :] = k_ref[...]


def norm_call(step, x, table, q_gain, k_gain):
    rows, width = x.shape
    cols = q_gain.shape[1]
    in_hbm = lambda array: pltpu.with_memory_space_constraint(array, pltpu.HBM)
    return pl.pallas_call(
        norm_kernel,
        in_specs=[SMEM] + [ANY] * 4,
        out_specs=[VMEM] * 3,
        out_shape=[
            jax.ShapeDtypeStruct((rows, width), jnp.bfloat16),
            jax.ShapeDtypeStruct((1, width), jnp.float32),
            jax.ShapeDtypeStruct((2, cols), jnp.float32),
        ],
        scratch_shapes=[
            pltpu.VMEM((rows, width), jnp.bfloat16),
            pltpu.VMEM((1, 3 * width), jnp.float32),
            pltpu.VMEM((1, cols), jnp.float32),
            pltpu.VMEM((1, cols), jnp.float32),
            pltpu.SemaphoreType.DMA((4,)),
        ],
        compiler_params=pltpu.CompilerParams(vmem_limit_bytes=8 * MIB),
        cost_estimate=pl.CostEstimate(flops=10 * rows * width, bytes_accessed=4 * rows * width, transcendentals=0),
    )(step, in_hbm(x), in_hbm(table), in_hbm(q_gain), in_hbm(k_gain))


def head_norm(values, gain):
    out = []
    for at in range(0, values.shape[1], HEAD_DIM):
        part = values[:, at : at + HEAD_DIM]
        power = jnp.mean(part * part, axis=-1, keepdims=True)
        out.append(part * lax.rsqrt(power + 1e-06) * gain[:, at : at + HEAD_DIM])
    return jnp.concatenate(out, axis=1)


def project(i, rows_ref, weights, gains, q_ref, kv_ref):
    owner, kind = divmod(i, 3)
    acc = jnp.dot(rows_ref[...], weights[owner][kind], preferred_element_type=jnp.float32)
    if kind < 2:
        gain = gains[1 + kind][...] if owner else gains[0][kind : kind + 1, :]
        acc = head_norm(acc, gain)
    if kind == 0:
        q_ref[owner] = acc.astype(jnp.bfloat16)
    else:
        kv_ref[2 * owner + kind - 1] = acc.astype(jnp.bfloat16)


def gather_rows(xs, rows_ref):
    at = 0
    for x in xs:
        rows_ref[at : at + x.shape[0], :] = x[...]
        at += x.shape[0]


def first_kernel(pieces, *refs):
    xs, gains = refs[:pieces], refs[pieces : pieces + 3]
    w_mine, w_other, q_ref, kv_ref, held, rows_ref, sems = refs[pieces + 3 :]
    copies = []
    for i in range(3):
        copies.append(pltpu.make_async_copy(w_mine.at[i], held.at[i], sems.at[i]))
        copies[i].start()
    gather_rows(xs, rows_ref)
    for i in (3, 4, 5, 0, 1, 2):
        if i < 3:
            copies[i].wait()
        project(i, rows_ref, (held, w_other), gains, q_ref, kv_ref)


def rest_keys_kernel(pieces, *refs):
    xs, gains = refs[:pieces], refs[pieces : pieces + 3]
    held, w_other, kv_ref, rows_ref = refs[pieces + 3 :]
    gather_rows(xs, rows_ref)
    for i in (1, 2, 4, 5):
        project(i, rows_ref, (held, w_other), gains, None, kv_ref)


def rest_queries_kernel(rows_ref, *refs):
    gains, (held, w_other, q_ref) = refs[:3], refs[3:]
    for i in (0, 3):
        project(i, rows_ref, (held, w_other), gains, q_ref, None)


def qkv_shapes(total, cols):
    return [
        jax.ShapeDtypeStruct((2, total, cols), jnp.bfloat16),
        jax.ShapeDtypeStruct((4, total, cols), jnp.bfloat16),
    ]


def first_call(xs, gains, w_mine, w_other):
    pieces = len(xs)
    width = xs[0].shape[1]
    total, cols = sum(x.shape[0] for x in xs), w_mine.shape[2]
    return pl.pallas_call(
        functools.partial(first_kernel, pieces),
        in_specs=[VMEM] * (pieces + 3) + [ANY, VMEM],
        out_specs=[VMEM] * 3,
        out_shape=qkv_shapes(total, cols) + [pltpu.VMEM((3, width, cols), jnp.bfloat16)],
        scratch_shapes=[pltpu.VMEM((total, width), jnp.bfloat16), pltpu.SemaphoreType.DMA((3,))],
        compiler_params=pltpu.CompilerParams(vmem_limit_bytes=24 * MIB),
        cost_estimate=pl.CostEstimate(
            flops=40 * 12 * total * width * cols, bytes_accessed=12 * width * cols, transcendentals=0
        ),
    )(
        *xs,
        *gains,
        pltpu.with_memory_space_constraint(w_mine, pltpu.HBM),
        pltpu.with_memory_space_constraint(w_other, pltpu.VMEM),
    )


def rest_call(xs, gains, held, w_other):
    pieces = len(xs)
    width = xs[0].shape[1]
    total, cols = sum(x.shape[0] for x in xs), held.shape[2]
    in_vmem = lambda array: pltpu.with_memory_space_constraint(array, pltpu.VMEM)
    params = pltpu.CompilerParams(vmem_limit_bytes=24 * MIB)
    cost = lambda count: pl.CostEstimate(
        flops=2 * count * total * width * cols, bytes_accessed=2 * count * width * cols, transcendentals=0
    )
    q_shape, kv_shape = qkv_shapes(total, cols)
    kv, rows = pl.pallas_call(
        functools.partial(rest_keys_kernel, pieces),
        in_specs=[VMEM] * (pieces + 5),
        out_specs=[VMEM] * 2,
        out_shape=[kv_shape, jax.ShapeDtypeStruct((total, width), jnp.bfloat16)],
        compiler_params=params,
        cost_estimate=cost(4),
    )(*xs, *gains, in_vmem(held), in_vmem(w_other))
    q = pl.pallas_call(
        rest_queries_kernel,
        in_specs=[VMEM] * 6,
        out_specs=VMEM,
        out_shape=q_shape,
        compiler_params=params,
        cost_estimate=cost(2),
    )(in_vmem(rows), *gains, in_vmem(held), in_vmem(w_other))
    return q, kv


def attend(q_ref, kv_ref, attn_ref):
    cols = q_ref.shape[2]
    contract = (((1,), (1,)), ((), ()))
    for owner in range(2):
        for at in range(0, cols, HEAD_DIM):
            span = slice(at, at + HEAD_DIM)
            scores = lax.dot_general(
                q_ref[owner, :, span], kv_ref[2 * owner, :, span], contract, preferred_element_type=jnp.float32
            ) * HEAD_DIM ** (-0.5)
            top = jnp.max(scores, axis=-1, keepdims=True)
            expo = jnp.exp(scores - top)
            total = jnp.sum(expo, axis=-1, keepdims=True)
            prob = (expo * (1.0 / total)).astype(jnp.bfloat16)
            value = jnp.dot(prob, kv_ref[2 * owner + 1, :, span], preferred_element_type=jnp.float32)
            attn_ref[:, owner * cols + at : owner * cols + at + HEAD_DIM] = value.astype(jnp.bfloat16)


def out_project(attn_ref, w_mine, w_other, outs):
    cols, width = w_mine.shape
    block = 1024
    for start in range(0, width, block):
        span = slice(start, start + block)
        part = jnp.dot(attn_ref[:, :cols], w_mine[:, span], preferred_element_type=jnp.float32)
        part += jnp.dot(attn_ref[:, cols:], w_other[:, span], preferred_element_type=jnp.float32)
        part = part.astype(jnp.bfloat16)
        at = 0
        for out in outs:
            out[:, span] = part[at : at + out.shape[0], :]
            at += out.shape[0]


def far_kernel(pieces, q_b, kv_a, kv_b, far_a, far_b, w_mine, w_other, *refs):
    outs, (kv_ref, attn_ref) = refs[:pieces], refs[pieces:]
    cut, most = kv_a.shape[1], kv_b.shape[1]
    half = cut + most
    for owner in range(2):
        for kind in range(2):
            near, far = 2 * owner + kind, 2 * (1 - owner) + kind
            kv_ref[near, :cut, :] = kv_a[near]
            kv_ref[near, cut:half, :] = kv_b[near]
            kv_ref[near, half : half + cut, :] = far_a[far]
            kv_ref[near, half + cut :, :] = far_b[far]
    attend(q_b, kv_ref, attn_ref)
    out_project(attn_ref, w_mine, w_other, outs)


def near_kernel(pieces, q_ref, kv_ref, w_mine, w_other, *refs):
    outs, attn_ref = refs[:pieces], refs[pieces]
    attend(q_ref, kv_ref, attn_ref)
    out_project(attn_ref, w_mine, w_other, outs)


def attend_call(kernel, operands, w_mine, w_other, sizes, length, keys=None):
    cols, width = w_mine.shape
    total = sum(sizes)
    out_shape = [jax.ShapeDtypeStruct((rows, width), jnp.bfloat16) for rows in sizes]
    if keys is not None:
        out_shape = out_shape + [jax.ShapeDtypeStruct(keys, jnp.bfloat16)]
    in_vmem = lambda array: pltpu.with_memory_space_constraint(array, pltpu.VMEM)
    return pl.pallas_call(
        functools.partial(kernel, len(sizes)),
        in_specs=[VMEM] * (len(operands) + 2),
        out_specs=[VMEM] * len(out_shape),
        out_shape=out_shape,
        scratch_shapes=[pltpu.VMEM((total, 2 * cols), jnp.bfloat16)],
        compiler_params=pltpu.CompilerParams(vmem_limit_bytes=24 * MIB),
        cost_estimate=pl.CostEstimate(
            flops=4 * total * cols * width + 8 * total * length * cols,
            bytes_accessed=4 * cols * width,
            transcendentals=4 * total * length,
        ),
    )(*operands, in_vmem(w_mine), in_vmem(w_other))


def body(latents, steps, leaving, fresh, mod_table, w_qkv, q_gain, k_gain, w_out):
    _, frames, local_rows, width = latents.shape
    rows = frames * local_rows
    own = latents.reshape(rows, width)
    normed, gate, gain = norm_call(steps, own, mod_table, q_gain[None], k_gain[None])

    w_mine = w_qkv.transpose(1, 0, 2)
    q_other, k_other = hop(q_gain[None], dc=1), hop(k_gain[None], dc=1)
    gains = [gain, q_other, k_other]
    w_send, _, _, _ = lax.optimization_barrier((w_mine, q_other, k_other, normed))
    w_other = hop(w_send, dc=1)

    left = hop(normed, dx=1)
    right = hop(normed, dx=-1)
    far = hop(normed, dz=1)
    across_send, _ = lax.optimization_barrier((normed, left))
    across = [hop(across_send, dx=2)]
    far_left = hop(left, dz=1)
    far_right = hop(right, dz=1)
    far_send, out_send, _ = lax.optimization_barrier((far, w_out, w_other))
    far_across = hop(far_send, dx=2)

    out_other = hop(out_send, dc=1)

    q_a, kv_a, held = first_call([normed, left, right, far], gains, w_mine, w_other)
    far_a = hop(kv_a, dc=1)
    q_b, kv_b = rest_call([far_left, far_right, far_across, *across], gains, held, w_other)
    far_b = hop(kv_b, dc=1)
    keys = (4, 16 * rows, kv_a.shape[2])
    half = rows // 2
    p_far_left, p_far_right, p_far_across, p_before, p_after, kv = attend_call(
        far_kernel, (q_b, kv_a, kv_b, far_a, far_b), w_out, out_other, [rows] * 3 + [half] * 2, keys[1], keys
    )
    p_own, p_left, p_right, p_far = attend_call(near_kernel, (q_a, kv), w_out, out_other, [rows] * 4, keys[1])

    def add(a, b):
        return (a.astype(jnp.float32) + b.astype(jnp.float32)).astype(jnp.bfloat16)

    def add_part(a, b, part, at):
        total = a.astype(jnp.float32) + b.astype(jnp.float32)
        part = part.astype(jnp.float32)
        halves = (total[: rows // 2], total[rows // 2 :])
        halves = (halves[0] + part, halves[1]) if at == 0 else (halves[0], halves[1] + part)
        return jnp.concatenate(halves, axis=0).astype(jnp.bfloat16)

    s_right = add_part(p_right, hop(p_far_right, dz=1), hop(p_before, dx=1), 0)
    s_left = add_part(p_left, hop(p_far_left, dz=1), hop(p_after, dx=-1), 1)
    s_far = add(p_far, hop(p_far_across, dx=2))
    arrived = [hop(s_left, dx=-1), hop(s_right, dx=1), hop(s_far, dz=1)]
    proj = p_own.astype(jnp.float32)
    for piece in arrived:
        proj = proj + piece.astype(jnp.float32)

    updated = (own.astype(jnp.float32) + gate * proj).astype(jnp.bfloat16).reshape(frames, local_rows, width)
    handed = lax.dynamic_slice_in_dim(updated, leaving[0], 1, axis=0)[0]
    arriving = from_behind(handed, "queue", 1)
    first = jnp.where(lax.axis_index("queue") == 0, fresh, arriving)
    return lax.dynamic_update_slice_in_dim(updated, first[None], leaving[0], axis=0)[None]


def solution(mesh):
    return jax.shard_map(
        body,
        mesh=mesh,
        in_specs=(
            P("queue", None, "seq", None),
            P("queue"),
            P("queue"),
            P("seq", None),
            P(),
            P(None, None, "seq"),
            P("seq"),
            P("seq"),
            P("seq", None),
        ),
        out_specs=P("queue", None, "seq", None),
        check_vma=False,
    )
```

```python
import functools

import jax
import jax.numpy as jnp
from jax import lax
from jax.experimental import pallas as pl
from jax.experimental.pallas import tpu as pltpu
from jax.sharding import PartitionSpec as P

HEAD_DIM = 128
EXP2_SCALE = HEAD_DIM**-0.5 * 1.4426950408889634
Z_CHIPS, X_CHIPS, CORES = 2, 4, 2
MIB = 1 << 20
ANY = pl.BlockSpec(memory_space=pl.ANY)
VMEM = pl.BlockSpec(memory_space=pltpu.VMEM)
SMEM = pl.BlockSpec(memory_space=pltpu.SMEM)


def hop(value, dz=0, dx=0, dc=0):
    pairs = []
    for z in range(Z_CHIPS):
        for x in range(X_CHIPS):
            for c in range(CORES):
                to_z, to_x, to_c = (z + dz) % Z_CHIPS, (x + dx) % X_CHIPS, (c + dc) % CORES
                pairs.append(((z * X_CHIPS + x) * CORES + c, (to_z * X_CHIPS + to_x) * CORES + to_c))
    return lax.ppermute(value, "seq", pairs)


def from_behind(x, axis, by):
    count = lax.axis_size(axis)
    pairs = [(i, (i + by) % count) for i in range(count)]
    return lax.ppermute(x, axis, pairs)


def norm_kernel(step, x_hbm, table, q_hbm, k_hbm, out_ref, gate_ref, gain_ref, x_ref, row, q_ref, k_ref, sems):
    width = x_hbm.shape[-1]
    moves = [(x_hbm, x_ref), (table.at[pl.ds(step[0], 1), :], row), (q_hbm, q_ref), (k_hbm, k_ref)]
    copies = [pltpu.make_async_copy(src, dst, sems.at[i]) for i, (src, dst) in enumerate(moves)]
    for copy in copies:
        copy.start()
    copies[0].wait()
    values = x_ref[...].astype(jnp.float32)
    mean = jnp.mean(values, axis=-1, keepdims=True)
    centred = values - mean
    var = jnp.mean(centred * centred, axis=-1, keepdims=True)
    scaled = centred * lax.rsqrt(var + 1e-06)
    for copy in copies[1:]:
        copy.wait()
    shift, scale = row[:, :width], row[:, width : 2 * width]
    out_ref[...] = (scaled * (1.0 + scale) + shift).astype(jnp.bfloat16)
    gate_ref[...] = row[:, 2 * width :]
    gain_ref[0:1, :] = q_ref[...]
    gain_ref[1:2, :] = k_ref[...]


def norm_call(step, x, table, q_gain, k_gain):
    rows, width = x.shape
    cols = q_gain.shape[1]
    in_hbm = lambda array: pltpu.with_memory_space_constraint(array, pltpu.HBM)
    return pl.pallas_call(
        norm_kernel,
        in_specs=[SMEM] + [ANY] * 4,
        out_specs=[VMEM] * 3,
        out_shape=[
            jax.ShapeDtypeStruct((rows, width), jnp.bfloat16),
            jax.ShapeDtypeStruct((1, width), jnp.float32),
            jax.ShapeDtypeStruct((2, cols), jnp.float32),
        ],
        scratch_shapes=[
            pltpu.VMEM((rows, width), jnp.bfloat16),
            pltpu.VMEM((1, 3 * width), jnp.float32),
            pltpu.VMEM((1, cols), jnp.float32),
            pltpu.VMEM((1, cols), jnp.float32),
            pltpu.SemaphoreType.DMA((4,)),
        ],
        compiler_params=pltpu.CompilerParams(vmem_limit_bytes=8 * MIB),
        cost_estimate=pl.CostEstimate(flops=10 * rows * width, bytes_accessed=4 * rows * width, transcendentals=0),
    )(step, in_hbm(x), in_hbm(table), in_hbm(q_gain), in_hbm(k_gain))


def head_norm(values, gain):
    out = []
    for at in range(0, values.shape[1], HEAD_DIM):
        part = values[:, at : at + HEAD_DIM]
        power = jnp.mean(part * part, axis=-1, keepdims=True)
        out.append(part * lax.rsqrt(power + 1e-06) * gain[:, at : at + HEAD_DIM])
    return jnp.concatenate(out, axis=1)


def project(i, rows_ref, weights, gains, q_ref, kv_ref):
    owner, kind = divmod(i, 3)
    acc = jnp.dot(rows_ref[...], weights[owner][kind], preferred_element_type=jnp.float32)
    if kind < 2:
        gain = gains[1 + kind][...] if owner else gains[0][kind : kind + 1, :]
        acc = head_norm(acc, gain)
    if kind == 0:
        q_ref[owner] = acc.astype(jnp.bfloat16)
    else:
        kv_ref[2 * owner + kind - 1] = acc.astype(jnp.bfloat16)


def gather_rows(xs, rows_ref):
    at = 0
    for x in xs:
        rows_ref[at : at + x.shape[0], :] = x[...]
        at += x.shape[0]


def first_kernel(pieces, *refs):
    xs, gains = refs[:pieces], refs[pieces : pieces + 3]
    w_mine, w_other, q_ref, kv_ref, held, rows_ref, sems = refs[pieces + 3 :]
    copies = []
    for i in range(3):
        copies.append(pltpu.make_async_copy(w_mine.at[i], held.at[i], sems.at[i]))
        copies[i].start()
    gather_rows(xs, rows_ref)
    for i in (3, 4, 5, 0, 1, 2):
        if i < 3:
            copies[i].wait()
        project(i, rows_ref, (held, w_other), gains, q_ref, kv_ref)


def rest_keys_kernel(pieces, *refs):
    xs, gains = refs[:pieces], refs[pieces : pieces + 3]
    held, w_other, kv_ref, rows_ref = refs[pieces + 3 :]
    gather_rows(xs, rows_ref)
    for i in (1, 2, 4, 5):
        project(i, rows_ref, (held, w_other), gains, None, kv_ref)


def rest_queries_kernel(rows_ref, *refs):
    gains, (held, w_other, q_ref) = refs[:3], refs[3:]
    for i in (0, 3):
        project(i, rows_ref, (held, w_other), gains, q_ref, None)


def qkv_shapes(total, cols):
    return [
        jax.ShapeDtypeStruct((2, total, cols), jnp.bfloat16),
        jax.ShapeDtypeStruct((4, total, cols), jnp.bfloat16),
    ]


def first_call(xs, gains, w_mine, w_other):
    pieces = len(xs)
    width = xs[0].shape[1]
    total, cols = sum(x.shape[0] for x in xs), w_mine.shape[2]
    return pl.pallas_call(
        functools.partial(first_kernel, pieces),
        in_specs=[VMEM] * (pieces + 3) + [ANY, VMEM],
        out_specs=[VMEM] * 3,
        out_shape=qkv_shapes(total, cols) + [pltpu.VMEM((3, width, cols), jnp.bfloat16)],
        scratch_shapes=[pltpu.VMEM((total, width), jnp.bfloat16), pltpu.SemaphoreType.DMA((3,))],
        compiler_params=pltpu.CompilerParams(vmem_limit_bytes=24 * MIB),
        cost_estimate=pl.CostEstimate(
            flops=40 * 12 * total * width * cols, bytes_accessed=12 * width * cols, transcendentals=0
        ),
    )(
        *xs,
        *gains,
        pltpu.with_memory_space_constraint(w_mine, pltpu.HBM),
        pltpu.with_memory_space_constraint(w_other, pltpu.VMEM),
    )


def rest_call(xs, gains, held, w_other):
    pieces = len(xs)
    width = xs[0].shape[1]
    total, cols = sum(x.shape[0] for x in xs), held.shape[2]
    in_vmem = lambda array: pltpu.with_memory_space_constraint(array, pltpu.VMEM)
    params = pltpu.CompilerParams(vmem_limit_bytes=24 * MIB)
    cost = lambda count: pl.CostEstimate(
        flops=2 * count * total * width * cols, bytes_accessed=2 * count * width * cols, transcendentals=0
    )
    q_shape, kv_shape = qkv_shapes(total, cols)
    kv, rows = pl.pallas_call(
        functools.partial(rest_keys_kernel, pieces),
        in_specs=[VMEM] * (pieces + 5),
        out_specs=[VMEM] * 2,
        out_shape=[kv_shape, jax.ShapeDtypeStruct((total, width), jnp.bfloat16)],
        compiler_params=params,
        cost_estimate=cost(4),
    )(*xs, *gains, in_vmem(held), in_vmem(w_other))
    q = pl.pallas_call(
        rest_queries_kernel,
        in_specs=[VMEM] * 6,
        out_specs=VMEM,
        out_shape=q_shape,
        compiler_params=params,
        cost_estimate=cost(2),
    )(in_vmem(rows), *gains, in_vmem(held), in_vmem(w_other))
    return q, kv


def attend(q_ref, near_refs, far_refs, attn_ref):
    cols = q_ref.shape[2]
    contract = (((1,), (1,)), ((), ()))
    for owner in range(2):
        parts = [(ref, 2 * owner) for ref in near_refs] + [(ref, 2 * (1 - owner)) for ref in far_refs]
        for at in range(0, cols, HEAD_DIM):
            span = slice(at, at + HEAD_DIM)
            query = q_ref[owner, :, span]
            scores = jnp.concatenate(
                [
                    lax.dot_general(query, ref[i, :, span], contract, preferred_element_type=jnp.float32)
                    for ref, i in parts
                ],
                axis=1,
            )
            top = jnp.max(scores, axis=-1, keepdims=True)
            expo = jnp.exp2((scores - top) * EXP2_SCALE)
            total = jnp.sum(expo, axis=-1, keepdims=True)
            expo = expo.astype(jnp.bfloat16)
            value, start = 0.0, 0
            for ref, i in parts:
                rows = ref.shape[1]
                value += jnp.dot(
                    expo[:, start : start + rows], ref[i + 1, :, span], preferred_element_type=jnp.float32
                )
                start += rows
            attn_ref[:, owner * cols + at : owner * cols + at + HEAD_DIM] = (value * (1.0 / total)).astype(
                jnp.bfloat16
            )


def out_project(attn_ref, w_mine, w_other, outs):
    cols, width = w_mine.shape
    block = 1024
    for start in range(0, width, block):
        span = slice(start, start + block)
        part = jnp.dot(attn_ref[:, :cols], w_mine[:, span], preferred_element_type=jnp.float32)
        part += jnp.dot(attn_ref[:, cols:], w_other[:, span], preferred_element_type=jnp.float32)
        part = part.astype(jnp.bfloat16)
        at = 0
        for out in outs:
            out[:, span] = part[at : at + out.shape[0], :]
            at += out.shape[0]


def attend_kernel(q_ref, kv_a, kv_b, far_a, far_b, w_mine, w_other, *refs):
    outs, attn_ref = refs[:-1], refs[-1]
    attend(q_ref, (kv_a, kv_b), (far_a, far_b), attn_ref)
    out_project(attn_ref, w_mine, w_other, outs)


def attend_call(operands, w_mine, w_other, sizes, length):
    cols, width = w_mine.shape
    total = sum(sizes)
    out_shape = [jax.ShapeDtypeStruct((rows, width), jnp.bfloat16) for rows in sizes]
    in_vmem = lambda array: pltpu.with_memory_space_constraint(array, pltpu.VMEM)
    return pl.pallas_call(
        attend_kernel,
        in_specs=[VMEM] * (len(operands) + 2),
        out_specs=[VMEM] * len(out_shape),
        out_shape=out_shape,
        scratch_shapes=[pltpu.VMEM((total, 2 * cols), jnp.bfloat16)],
        compiler_params=pltpu.CompilerParams(vmem_limit_bytes=24 * MIB),
        cost_estimate=pl.CostEstimate(
            flops=4 * total * cols * width + 8 * total * length * cols,
            bytes_accessed=4 * cols * width,
            transcendentals=4 * total * length,
        ),
    )(*operands, in_vmem(w_mine), in_vmem(w_other))


def body(latents, steps, leaving, fresh, mod_table, w_qkv, q_gain, k_gain, w_out):
    _, frames, local_rows, width = latents.shape
    rows = frames * local_rows
    own = latents.reshape(rows, width)
    normed, gate, gain = norm_call(steps, own, mod_table, q_gain[None], k_gain[None])

    w_mine = w_qkv.transpose(1, 0, 2)
    q_other, k_other = hop(q_gain[None], dc=1), hop(k_gain[None], dc=1)
    gains = [gain, q_other, k_other]
    w_send, _, _, _ = lax.optimization_barrier((w_mine, q_other, k_other, normed))
    w_other = hop(w_send, dc=1)

    left = hop(normed, dx=1)
    right = hop(normed, dx=-1)
    far = hop(normed, dz=1)
    across_send, _ = lax.optimization_barrier((normed, left))
    across = [hop(across_send, dx=2)]
    far_left = hop(left, dz=1)
    far_right = hop(right, dz=1)
    far_send, out_send, _ = lax.optimization_barrier((far, w_out, w_other))
    far_across = hop(far_send, dx=2)

    out_other = hop(out_send, dc=1)

    q_a, kv_a, held = first_call([normed, left, right, far], gains, w_mine, w_other)
    far_a = hop(kv_a, dc=1)
    q_b, kv_b = rest_call([far_left, far_right, far_across, *across], gains, held, w_other)
    far_b = hop(kv_b, dc=1)
    half, length = rows // 2, 16 * rows
    keys = (kv_a, kv_b, far_a, far_b)
    p_far_left, p_far_right, p_far_across, p_before, p_after = attend_call(
        (q_b, *keys), w_out, out_other, [rows] * 3 + [half] * 2, length
    )
    p_own, p_left, p_right, p_far = attend_call((q_a, *keys), w_out, out_other, [rows] * 4, length)

    def add(a, b):
        return (a.astype(jnp.float32) + b.astype(jnp.float32)).astype(jnp.bfloat16)

    def add_part(a, b, part, at):
        total = a.astype(jnp.float32) + b.astype(jnp.float32)
        part = part.astype(jnp.float32)
        halves = (total[: rows // 2], total[rows // 2 :])
        halves = (halves[0] + part, halves[1]) if at == 0 else (halves[0], halves[1] + part)
        return jnp.concatenate(halves, axis=0).astype(jnp.bfloat16)

    s_right = add_part(p_right, hop(p_far_right, dz=1), hop(p_before, dx=1), 0)
    s_left = add_part(p_left, hop(p_far_left, dz=1), hop(p_after, dx=-1), 1)
    s_far = add(p_far, hop(p_far_across, dx=2))
    arrived = [hop(s_left, dx=-1), hop(s_right, dx=1), hop(s_far, dz=1)]
    proj = p_own.astype(jnp.float32)
    for piece in arrived:
        proj = proj + piece.astype(jnp.float32)

    updated = (own.astype(jnp.float32) + gate * proj).astype(jnp.bfloat16).reshape(frames, local_rows, width)
    handed = lax.dynamic_slice_in_dim(updated, leaving[0], 1, axis=0)[0]
    arriving = from_behind(handed, "queue", 1)
    first = jnp.where(lax.axis_index("queue") == 0, fresh, arriving)
    return lax.dynamic_update_slice_in_dim(updated, first[None], leaving[0], axis=0)[None]


def solution(mesh):
    return jax.shard_map(
        body,
        mesh=mesh,
        in_specs=(
            P("queue", None, "seq", None),
            P("queue"),
            P("queue"),
            P("seq", None),
            P(),
            P(None, None, "seq"),
            P("seq"),
            P("seq"),
            P("seq", None),
        ),
        out_specs=P("queue", None, "seq", None),
        check_vma=False,
    )
```
